32 devices in a mesh: dp: 4 (over y, core), mp: 8 (over z, x).
Axes of the slice: x: 2, y: 2, z: 4, core: 2. Of those that a mesh axis runs over, the one named last changes fastest.
Arguments:
- tokens: bfloat16 [4096, 2048], P(('dp', 'mp')), may hold values from -6 to 6
- norm_gain: float32 [2048], replicated, may hold values from 0.1 to 1.9
- router: bfloat16 [2048, 8], replicated, may hold values from -0.125 to 0.125
- routes: int32 [4096, 2], P(('dp', 'mp')), may hold values from 0 to 7, all different within a row; in each aligned block of 128 rows (0 to 127, 128 to 255, ...) at most 40 rows name the same one
- prompt_lengths: int32 [8], replicated, may hold values from 256 to 512, as said below
- wq_train: float32 [8, 2048, 2048], P(None, ('dp', 'mp'))
- wo_train: float32 [8, 2048, 2048], P(None, ('dp', 'mp')), may hold values from -0.25 to 0.25
- wkv_train: float32 [2048, 4096], P(('dp', 'mp')), as said below
- page_table: int32 [4, 8, 8], P('dp', 'mp'), may hold values from 0 to 127, as said below
Outputs:
- attn_out: bfloat16 [4096, 2048], P(('dp', 'mp'))
- kv_pool: bfloat16 [512, 16, 4096], P(('dp', 'mp'))
The draws below stay inside these ranges and needn't reach their ends.
Inputs may be any that keep to these rules, and one draw needn't show every extreme that they name: `routes`: each of the two entries of a row names a different expert; in the rows of one device (aligned blocks of 128 rows) no expert is named by more than 40 rows, a bound that some block reaches. `prompt_lengths`: every prompt uses at least 256 slots; some prompt uses all 512 and another exactly 256. `page_table`: entry [g, w, q] equals owner * 16 + w * 2 + c with c < 2; the pairs (owner, c) of one writer w in one group are distinct, so at most 2 pages of one writer go to one owner. In every group one owner receives 2 pages from every writer. Pool pages that no entry names stay zero. `wkv_train`: entries of order D^-1/2.
All inputs are finite; a program needn't handle non-finite values.
Results may differ from the reference program's by a relative error of at most 0.012.
The reference program's roundings to bfloat16 on the way count: a program that leaves them out, or rounds other values in their place, can miss the bound.
Values may be sent and summed in bfloat16 or wider, within the bound.
A program may use at most 192 MiB of HBM per device.

```python
import math
import jax
import jax.numpy as jnp
import numpy as np
from jax import lax

D = 2048
HEADS = 16
HD = 128
EXPERTS = 8
TOPK = 2
TOK_DEV = 128
PAGE = 16
PCAP = 2
PROMPTS = 8
LEN = 512
ROWS = 4096
HB = 16
CAP = 40
PW = 8
SLOTS = 16
N_DP = 4
N_MP = 8


def key_basis(key):
    return jax.random.normal(jax.random.fold_in(key, 31), (D, HEADS * HD), jnp.float32) * D ** (-0.5)


def draw_wkv_train(key, part):
    key_part = key_basis(key)
    value_part = jax.random.normal(jax.random.fold_in(key, 32), (D, HEADS * HD), jnp.float32) * D ** (-0.5)
    return jnp.concatenate([key_part, value_part], axis=1)


def draw_wq_train(key, part):
    noise = jax.random.normal(jax.random.fold_in(key, 33), (EXPERTS, D, HEADS * HD), jnp.float32)
    return noise * (3.0 * D ** (-0.5))


def draw_prompt_lengths(key, part):
    base_key = jax.random.fold_in(key, 21)
    length_key, long_key, short_key = jax.random.split(base_key, 3)
    shortest = LEN // 2
    lengths_drawn = jax.random.randint(length_key, (PROMPTS,), shortest, LEN + 1)
    longest_at = jax.random.randint(long_key, (), 0, PROMPTS)
    shortest_at = (longest_at + 1 + jax.random.randint(short_key, (), 0, PROMPTS - 1)) % PROMPTS
    indices = jnp.arange(PROMPTS)
    lengths_drawn = jnp.where(indices == longest_at, LEN, lengths_drawn)
    lengths_drawn = jnp.where(indices == shortest_at, shortest, lengths_drawn)
    return lengths_drawn.astype(jnp.int32)


def writer_row(writer_key, writer, hot_owner):
    page_order = jax.random.permutation(jax.random.fold_in(writer_key, 2), PW)
    page_ranks = jnp.zeros((PW,), jnp.int32).at[page_order].set(jnp.arange(PW, dtype=jnp.int32))
    spare_cells = jax.random.permutation(jax.random.fold_in(writer_key, 3), (N_MP - 1) * PCAP).astype(jnp.int32)
    cell_ids = jnp.concatenate([jnp.zeros((PCAP,), jnp.int32), spare_cells])[page_ranks]
    others_owner = cell_ids // PCAP
    others_owner = others_owner + (others_owner >= hot_owner).astype(jnp.int32)
    owner_ids = jnp.where(page_ranks < PCAP, hot_owner, others_owner)
    column = jnp.where(page_ranks < PCAP, page_ranks, cell_ids % PCAP)
    return owner_ids * SLOTS + writer * PCAP + column


def group_table(key, group_index):
    group_key = jax.random.fold_in(jax.random.fold_in(key, 41), group_index)
    hot_owner = jax.random.randint(jax.random.fold_in(group_key, 1), (), 0, N_MP)
    writers = jnp.arange(N_MP, dtype=jnp.int32)
    return jax.vmap(lambda writer: writer_row(jax.random.fold_in(group_key, 100 + writer), writer, hot_owner))(writers)


def draw_page_table(key, part):
    groups = jnp.arange(N_DP, dtype=jnp.int32)
    return jax.vmap(lambda group_index: group_table(key, group_index))(groups).astype(jnp.int32)


def shard_levels(own_key, dims, cuts, smallest, top_value):
    def one(position, blocks):
        steps = jax.random.uniform(jax.random.fold_in(jax.random.fold_in(own_key, 6), position), (blocks,), jnp.float32, smallest / len(cuts), top_value / len(cuts))
        return jnp.repeat(jnp.exp(steps), dims[position] // blocks).reshape((-1,) + (1,) * (len(dims) - position - 1))

    level = one(*cuts[0])
    for cut in cuts[1:]:
        level = level * one(*cut)
    return level


def deal_out(rng, own, number, rows, count, top, reach, skew):
    order = jax.random.permutation(rng, count)
    heavy_load, common = load_shares(count, rows * top, reach, skew, True), load_shares(count, rows * top, reach, skew, False)
    places = jnp.arange(count)

    def named(tallies, rotation):
        used = int((tallies > 0).sum())
        fixed = max(1, used // 4)
        passed = fixed + (places - fixed + rotation * (used - fixed)) % max(1, count - fixed)
        return jnp.zeros((count,), jnp.int32).at[order[jnp.where(places < fixed, places, passed)]].set(jnp.asarray(tallies, jnp.int32))

    tallies = jnp.where(number % 4 == 0, named(heavy_load, number // 4), named(common, number - number // 4 - 1))
    mixed = jax.random.permutation(jax.random.fold_in(own, 3), count)
    source_of, receiver = mixed[0:count // 2 * 2:2], mixed[1:count // 2 * 2:2]
    slack = jnp.minimum(tallies[source_of] - 1, reach - tallies[receiver]) // 2
    slack = jnp.where((source_of == order[0]) | (receiver == order[0]) | (tallies[receiver] == 0), 0, jnp.maximum(slack, 0))
    passed = jax.random.randint(jax.random.fold_in(own, 4), (count // 2,), 0, 1 << 20) % (slack + 1)
    tallies = tallies.at[source_of].add(-passed).at[receiver].add(passed)
    members = jnp.searchsorted(jnp.cumsum(tallies), jnp.arange(rows * top), side="right").astype(jnp.int32)
    table = members.reshape(top, rows).T
    table = table[jax.random.permutation(jax.random.fold_in(own, 1), rows)]
    rotation = jax.random.randint(jax.random.fold_in(own, 2), (rows, 1), 0, top)
    return jnp.take_along_axis(table, (jnp.arange(top)[None, :] + rotation) % top, axis=1)


def load_shares(count, total, reach, slope, full):
    weights = [(1 << 20) // math.isqrt(grade ** slope) + 1 for grade in range(1, count + 1)]
    largest = reach if full else min(reach, max(-(-total // count), total * weights[0] // sum(weights)))
    least = 1 if total - largest >= count - 1 else 0
    given, spare = [largest] + [least] * (count - 1), total - largest - least * (count - 1)
    while spare > 0:
        candidates = [i for i in range(1, count) if given[i] < largest] or [i for i in range(1, count) if given[i] < reach]
        whole, remaining = sum([weights[i] for i in candidates]), spare
        for i in candidates:
            addition = min(reach - given[i], max(1, remaining * weights[i] // whole), spare)
            given[i] = given[i] + addition
            spare = spare - addition
    return np.array(given)


def normal_values(own_key, extent, deviation, most, cuts=(), held_as=jnp.bfloat16):
    array = jax.random.normal(own_key, extent, jnp.float32) * deviation
    if len(cuts) > 0:
        array = shard_levels(own_key, extent, cuts, -0.22, 0.18) * array
    return jnp.clip(array, min=-most, max=most).astype(held_as)


def setup_inputs(seed: int = 0) -> dict:
    streams_of = jax.random.split(jax.random.key(seed), 10)
    tokens = normal_values(streams_of[0], (ROWS, D), 1.0, 6.0, ((0, 32),))
    norm_gain = jnp.clip(1.0 + 0.18 * jax.random.normal(streams_of[1], (D,), jnp.float32), 0.1, 1.9)
    router = normal_values(streams_of[2], (D, EXPERTS), D ** -0.5, 0.125)
    routes_keys = jax.random.split(jax.random.fold_in(streams_of[3], 1), ROWS // TOK_DEV)
    routes_turns = jax.random.permutation(jax.random.fold_in(streams_of[3], 3), ROWS // TOK_DEV)
    routes = jax.vmap(lambda own, number: deal_out(jax.random.fold_in(streams_of[3], 2), own, number, TOK_DEV, EXPERTS, TOPK, CAP, 2))(routes_keys, routes_turns).reshape((ROWS, TOPK))
    prompt_lengths = draw_prompt_lengths(jax.random.fold_in(streams_of[9], 71), 0)
    wq_train = draw_wq_train(jax.random.fold_in(streams_of[9], 71), 0)
    wo_train = normal_values(streams_of[6], (EXPERTS, D, HEADS * HD), (HEADS * HD // 4) ** -0.5, 0.25, ((1, 32),), jnp.float32)
    wkv_train = draw_wkv_train(jax.random.fold_in(streams_of[9], 71), 0)
    page_table = draw_page_table(jax.random.fold_in(streams_of[9], 71), 0)
    return {"tokens": tokens, "norm_gain": norm_gain, "router": router, "routes": routes, "prompt_lengths": prompt_lengths, "wq_train": wq_train, "wo_train": wo_train, "wkv_train": wkv_train, "page_table": page_table}


def rotate(vectors, positions):
    half_dim = vectors.shape[-1] // 2
    frequency = 10000.0 ** (-(jnp.arange(half_dim, dtype=jnp.float32) * 2.0 / vectors.shape[-1]))
    angles = positions.astype(jnp.float32)[:, None] * frequency[None, :]
    cosine = jnp.cos(angles)[:, None, :]
    sine = jnp.sin(angles)[:, None, :]
    leading = vectors[..., :half_dim]
    trailing = vectors[..., half_dim:]
    return jnp.concatenate([leading * cosine - trailing * sine, trailing * cosine + leading * sine], axis=-1)

def page_view(matrix):
    block_count = N_MP // EXPERTS
    block_width = HB * HD
    shaped = matrix.reshape(N_DP, EXPERTS, PW, PAGE, block_count, block_width)
    return shaped.transpose(0, 1, 4, 2, 3, 5).reshape(N_DP, N_MP, PW, PAGE, block_width)

def reference(tokens, norm_gain, router, routes, prompt_lengths, wq_train, wo_train, wkv_train, page_table):
    width = HEADS * HD
    block_width = HB * HD
    block_count = N_MP // EXPERTS
    query_count = N_MP // 2 * CAP
    server_query = wq_train.astype(jnp.bfloat16)
    server_output = wo_train.astype(jnp.bfloat16)
    server_pair = wkv_train.astype(jnp.bfloat16)
    wide_tokens = tokens.astype(jnp.float32)
    normed = (wide_tokens * lax.rsqrt(lax.optimization_barrier(jnp.mean(wide_tokens * wide_tokens, axis=-1, keepdims=True)) + 1e-06) * norm_gain).astype(jnp.bfloat16)
    positions = jnp.arange(ROWS, dtype=jnp.int32) % LEN
    projected = jnp.dot(normed, server_pair, preferred_element_type=jnp.float32)
    key_rows = rotate(projected[:, :width].reshape(ROWS, HEADS, HD), positions).reshape(ROWS, width).astype(jnp.bfloat16)
    value_rows = projected[:, width:].astype(jnp.bfloat16)
    content = jnp.concatenate([page_view(key_rows), page_view(value_rows)], axis=-1)
    page_ids = page_table + (jnp.arange(N_DP, dtype=jnp.int32) * (N_MP * SLOTS))[:, None, None]
    page_pool = jnp.zeros((N_DP * N_MP * SLOTS, PAGE, 2 * block_width), jnp.bfloat16)
    page_pool = page_pool.at[page_ids.reshape(-1)].set(content.reshape(-1, PAGE, 2 * block_width))
    logits = jnp.dot(normed, router, preferred_element_type=jnp.float32)
    first_pick = routes[:, 0]
    second_pick = routes[:, 1]
    first_logit = jnp.take_along_axis(logits, routes[:, 0:1], axis=1)[:, 0]
    second_logit = jnp.take_along_axis(logits, routes[:, 1:2], axis=1)[:, 0]
    gate_first = 1.0 / (1.0 + jnp.exp(second_logit - first_logit))
    gate_second = 1.0 / (1.0 + jnp.exp(first_logit - second_logit))
    key_heads = key_rows.reshape(PROMPTS, LEN, HEADS, HD)
    value_heads = value_rows.reshape(PROMPTS, LEN, HEADS, HD)
    slot_index = jnp.arange(CAP, dtype=jnp.int32)
    local_rows = jnp.arange(TOK_DEV, dtype=jnp.int32)
    key_index = jnp.arange(LEN, dtype=jnp.int32)
    owner_start = jnp.arange(N_DP * N_MP, dtype=jnp.int32)[:, None] * TOK_DEV

    def expert_term(operands):
        expert, query_weight, output_weight = operands
        named = ((first_pick == expert) | (second_pick == expert)).reshape(N_DP * N_MP, TOK_DEV)
        ranking = jnp.cumsum(named.astype(jnp.int32), axis=1) - 1
        chosen = named[:, None, :] & (ranking[:, None, :] == slot_index[None, :, None])
        slot_row = (lax.optimization_barrier(jnp.sum(jnp.where(chosen, local_rows[None, None, :], 0), axis=-1)) + owner_start).reshape(-1).astype(jnp.int32)
        filled = jnp.any(chosen, axis=-1).reshape(-1)
        queries = jnp.dot(normed[slot_row], query_weight, preferred_element_type=jnp.float32).reshape(-1, HEADS, HD)
        queries = (rotate(queries, positions[slot_row]) * HD ** (-0.5)).astype(jnp.bfloat16)
        query_heads = queries.reshape(PROMPTS, query_count, HEADS, HD)
        query_places = positions[slot_row].reshape(PROMPTS, query_count)

        def prompt_attention(inputs):
            query_block, places, key_block, value_block, length = inputs
            scores = jnp.einsum('qhd,khd->hqk', query_block.astype(jnp.float32), key_block.astype(jnp.float32))
            allowed = (key_index[None, :] <= places[:, None]) & (key_index[None, :] < length)
            scores = jnp.where(allowed[None], scores, -jnp.inf)
            highest = lax.optimization_barrier(jnp.max(scores, axis=-1, keepdims=True))
            powered = jnp.exp(scores - highest)
            softened = (powered / lax.optimization_barrier(jnp.sum(powered, axis=-1, keepdims=True))).astype(jnp.bfloat16)
            return jnp.einsum('hqk,khd->qhd', softened.astype(jnp.float32), value_block.astype(jnp.float32)).astype(jnp.bfloat16)
        heads_out = lax.map(prompt_attention, (query_heads, query_places, key_heads, value_heads, prompt_lengths))
        heads_out = heads_out.reshape(-1, block_count, block_width)
        blocked_output = output_weight.reshape(D, block_count, block_width)
        partial_value = jnp.einsum('nbk,dbk->nbd', heads_out.astype(jnp.float32), blocked_output.astype(jnp.float32)).astype(jnp.bfloat16)
        summed = lax.optimization_barrier(jnp.sum(partial_value.astype(jnp.float32), axis=1))
        gate = jnp.where(first_pick[slot_row] == expert, gate_first[slot_row], gate_second[slot_row])
        gate = jnp.where(filled, gate, 0.0)
        return (gate[:, None] * summed, slot_row)
    terms, targets = lax.map(expert_term, (jnp.arange(EXPERTS, dtype=jnp.int32), server_query, server_output))
    mixed = jnp.zeros((ROWS, D), jnp.float32).at[targets.reshape(-1)].add(terms.reshape(-1, D))
    return (mixed.astype(jnp.bfloat16), page_pool)
```

```python
import functools

import jax
import jax.numpy as jnp
from jax import lax
from jax.experimental import pallas as pl
from jax.experimental.pallas import tpu as pltpu
from jax.sharding import PartitionSpec as P

HD = 128
PAGE = 16
PCAP = 2


def rotate(vectors, positions):
    half_dim = vectors.shape[-1] // 2
    frequency = 10000.0 ** (-(jnp.arange(half_dim, dtype=jnp.float32) * 2.0 / vectors.shape[-1]))
    angles = positions.astype(jnp.float32)[:, None] * frequency[None, :]
    cosine = jnp.cos(angles)[:, None, :]
    sine = jnp.sin(angles)[:, None, :]
    leading = vectors[..., :half_dim]
    trailing = vectors[..., half_dim:]
    return jnp.concatenate(
        [leading * cosine - trailing * sine, trailing * cosine + leading * sine], axis=-1
    )


def by_expert(
    tokens, norm_gain, router, routes, prompt_lengths, wq_train, wo_train, wkv_train, page_table
):
    mp_count = lax.axis_size("mp")
    experts = wq_train.shape[0]
    blocks = mp_count // experts
    width = wq_train.shape[2]
    block_width = width // blocks
    head_dim = HD
    block_heads = block_width // head_dim
    tok_rows = tokens.shape[0]
    model_width = tokens.shape[1]
    capacity = tok_rows // 4 + tok_rows // 16
    prompt_len = tok_rows * mp_count // 2
    writer_pages = tok_rows * blocks // PAGE
    slot_count = mp_count * PCAP
    device = lax.axis_index("mp")
    expert = device // blocks
    prompt_group = lax.axis_index("dp")
    shard_rows = wq_train.shape[1]
    query_part = wq_train.reshape(experts, shard_rows, blocks, block_width).transpose(0, 2, 1, 3)
    query_part = query_part.reshape(mp_count, shard_rows, block_width).astype(jnp.bfloat16)
    output_part = wo_train.reshape(experts, shard_rows, blocks, block_width).transpose(0, 2, 1, 3)
    output_part = output_part.reshape(mp_count, shard_rows, block_width).astype(jnp.bfloat16)
    pair_part = wkv_train.reshape(shard_rows, 2, blocks, block_width).transpose(2, 0, 1, 3)
    pair_part = pair_part.reshape(blocks, shard_rows, 2 * block_width)
    pair_part = jnp.broadcast_to(pair_part[None], (experts, blocks, shard_rows, 2 * block_width))
    pair_part = pair_part.reshape(mp_count, shard_rows, 2 * block_width).astype(jnp.bfloat16)
    exchanged = (
        lax.all_to_all(query_part, "mp", split_axis=0, concat_axis=1, tiled=True),
        lax.all_to_all(output_part, "mp", split_axis=0, concat_axis=1, tiled=True),
        lax.all_to_all(pair_part, "mp", split_axis=0, concat_axis=1, tiled=True),
    )
    query_w, output_w, pair_w = (
        lax.all_gather(exchanged[0], "dp", axis=1, tiled=True),
        lax.all_gather(exchanged[1], "dp", axis=1, tiled=True),
        lax.all_gather(exchanged[2], "dp", axis=1, tiled=True),
    )
    query_w = query_w[0]
    output_w = output_w[0]
    pair_w = pair_w[0]
    wide_tokens = tokens.astype(jnp.float32)
    normed = (
        wide_tokens
        * lax.rsqrt(jnp.mean(wide_tokens * wide_tokens, axis=-1, keepdims=True) + 1e-06)
        * norm_gain
    ).astype(jnp.bfloat16)
    logits = jnp.dot(normed, router, preferred_element_type=jnp.float32)
    labels = jnp.arange(experts, dtype=jnp.int32)
    first_hot = routes[:, 0][None, :] == labels[:, None]
    second_hot = routes[:, 1][None, :] == labels[:, None]
    first_logit = jnp.sum(jnp.where(first_hot.T, logits, 0.0), axis=1)
    second_logit = jnp.sum(jnp.where(second_hot.T, logits, 0.0), axis=1)
    gate_first = 1.0 / (1.0 + jnp.exp(second_logit - first_logit))
    gate_second = 1.0 / (1.0 + jnp.exp(first_logit - second_logit))
    gates = jnp.where(
        first_hot, gate_first[None, :], jnp.where(second_hot, gate_second[None, :], 0.0)
    )
    named = first_hot | second_hot
    upto = jnp.arange(tok_rows)[:, None] <= jnp.arange(tok_rows)[None, :]
    ranking = (
        jnp.dot(
            named.astype(jnp.bfloat16),
            upto.astype(jnp.bfloat16),
            preferred_element_type=jnp.float32,
        ).astype(jnp.int32)
        - 1
    )
    chosen = named[:, None, :] & (
        ranking[:, None, :] == jnp.arange(capacity, dtype=jnp.int32)[None, :, None]
    )
    slot_row = jnp.sum(
        jnp.where(chosen, jnp.arange(tok_rows, dtype=jnp.int32)[None, None, :], 0), axis=-1
    )
    filled = jnp.any(chosen, axis=-1)
    picked = jnp.where(filled[..., None], normed[slot_row], jnp.zeros((), jnp.bfloat16))
    outgoing = jnp.broadcast_to(picked[:, None], (experts, blocks, capacity, model_width)).reshape(
        mp_count, capacity, model_width
    )
    places = jnp.where(filled, (device * tok_rows + slot_row) % prompt_len, 0)
    outgoing_places = jnp.broadcast_to(places[:, None], (experts, blocks, capacity)).reshape(
        mp_count, capacity
    )
    arrived = lax.all_to_all(outgoing, "mp", split_axis=0, concat_axis=0, tiled=True)
    arrived_places = lax.all_to_all(outgoing_places, "mp", split_axis=0, concat_axis=0, tiled=True)
    segment = lax.all_gather(normed, "mp", axis=0, tiled=True)
    projected = jnp.dot(segment, pair_w, preferred_element_type=jnp.float32)
    row_places = jnp.arange(segment.shape[0], dtype=jnp.int32) % prompt_len
    keyed = rotate(
        projected[:, :block_width].reshape(-1, block_heads, head_dim), row_places
    ).reshape(-1, block_width)
    kv_rows = jnp.concatenate([keyed, projected[:, block_width:]], axis=1).astype(jnp.bfloat16)
    own_pages = lax.dynamic_slice_in_dim(
        kv_rows, expert * writer_pages * PAGE, writer_pages * PAGE, 0
    )
    own_pages = own_pages.reshape(writer_pages, PAGE, 2 * block_width)
    page_ids = page_table[0, 0]
    target_cells = page_ids // slot_count * PCAP + page_ids % PCAP
    placing = (
        target_cells[None, :] == jnp.arange(mp_count * PCAP, dtype=jnp.int32)[:, None]
    ).astype(jnp.bfloat16)
    outgoing_pages = jnp.einsum(
        "cq,qpk->cpk", placing, own_pages, preferred_element_type=jnp.float32
    ).astype(jnp.bfloat16)
    outgoing_pages = outgoing_pages.reshape(mp_count, PCAP, PAGE, 2 * block_width)
    page_pool = lax.all_to_all(outgoing_pages, "mp", split_axis=0, concat_axis=0, tiled=True)
    queries = jnp.dot(arrived.reshape(-1, model_width), query_w, preferred_element_type=jnp.float32)
    query_places = arrived_places.reshape(-1)
    queries = (
        rotate(queries.reshape(-1, block_heads, head_dim), query_places) * head_dim ** (-0.5)
    ).astype(jnp.bfloat16)
    key_side = (
        kv_rows[:, :block_width].reshape(2, prompt_len, block_heads, head_dim).transpose(0, 2, 1, 3)
    )
    value_side = (
        kv_rows[:, block_width:].reshape(2, prompt_len, block_heads, head_dim).transpose(0, 2, 1, 3)
    )
    key_index = jnp.arange(prompt_len, dtype=jnp.int32)
    half_rows = mp_count // 2 * capacity
    sides = []
    for side in range(2):
        side_places = query_places[side * half_rows : (side + 1) * half_rows]
        length = prompt_lengths[2 * prompt_group + side]
        allowed = (key_index[None, :] <= side_places[:, None]) & (key_index[None, :] < length)
        side_queries = queries[side * half_rows : (side + 1) * half_rows].transpose(1, 0, 2)

        def one_head(operands):
            query_head, key_head, value_head = operands
            scores = lax.dot_general(
                query_head, key_head, (((1,), (1,)), ((), ())), preferred_element_type=jnp.float32
            )
            scores = jnp.where(allowed, scores, -jnp.inf)
            highest = jnp.max(scores, axis=-1, keepdims=True)
            powered = jnp.exp(scores - highest)
            softened = (powered / jnp.sum(powered, axis=-1, keepdims=True)).astype(jnp.bfloat16)
            return jnp.dot(softened, value_head, preferred_element_type=jnp.float32).astype(
                jnp.bfloat16
            )

        sides.append(lax.map(one_head, (side_queries, key_side[side], value_side[side])))
    heads_out = jnp.stack(sides).transpose(0, 2, 1, 3).reshape(2 * half_rows, block_width)
    partial_value = lax.dot_general(
        heads_out, output_w, (((1,), (1,)), ((), ())), preferred_element_type=jnp.float32
    )
    partial_value = partial_value.astype(jnp.bfloat16).reshape(mp_count, capacity, model_width)
    returned = lax.all_to_all(partial_value, "mp", split_axis=0, concat_axis=0, tiled=True)
    page_pool = page_pool.reshape(slot_count, PAGE, 2 * block_width)
    summed = (
        returned.astype(jnp.float32).reshape(experts, blocks, capacity, model_width).sum(axis=1)
    )
    summed = summed.reshape(experts * capacity, model_width)
    weights = jnp.where(chosen, gates[:, None, :], 0.0).reshape(experts * capacity, tok_rows)
    mixed = lax.dot_general(
        weights,
        summed,
        (((0,), (0,)), ((), ())),
        precision=lax.Precision.HIGHEST,
        preferred_element_type=jnp.float32,
    )
    return (mixed.astype(jnp.bfloat16), page_pool)


def turned(vectors, cosine, sine):
    return vectors * cosine + pltpu.roll(vectors, vectors.shape[-1] // 2, 1) * sine


def pages_kernel(heads, source_ref, raw_ref, cosine_ref, sine_ref, kv_ref, pool_ref):
    rows = raw_ref.shape[0]
    width = heads * HD
    for h in range(heads):
        columns = slice(h * HD, (h + 1) * HD)
        kv_ref[:, columns] = turned(
            raw_ref[:, columns], cosine_ref[...], sine_ref[...]
        ).astype(jnp.bfloat16)
    kv_ref[:, width:] = raw_ref[:, width:].astype(jnp.bfloat16)

    def place(cell, carry):
        page = source_ref[cell]
        start = pl.multiple_of(jnp.maximum(page, 0) * PAGE, PAGE)
        content = kv_ref[pl.ds(start, PAGE), :]
        pool_ref[pl.ds(pl.multiple_of(cell * PAGE, PAGE), PAGE), :] = jnp.where(
            page >= 0, content, jnp.zeros_like(content)
        )
        return carry

    lax.fori_loop(0, pool_ref.shape[0] // PAGE, place, 0)


def attention_kernel(
    experts, length_ref, raw_ref, key_ref, value_ref, cosine_ref, sine_ref, side_ref, out_ref
):
    rows = key_ref.shape[0]
    length = length_ref[pl.program_id(0)]
    key_index = lax.broadcasted_iota(jnp.int32, (rows, rows), 1)
    row_index = lax.broadcasted_iota(jnp.int32, (rows, rows), 0)
    allowed = (key_index <= row_index) & (key_index < length)
    keys = key_ref[...]
    values = value_ref[...]
    mixed = []
    names = []
    for choice in range(2):
        name = side_ref[:, choice : choice + 1]
        gate = side_ref[:, 2 + choice : 3 + choice]
        query = jnp.zeros((rows, HD), jnp.float32)
        for e in range(experts):
            query = jnp.where(name == float(e), raw_ref[:, e * HD : (e + 1) * HD], query)
        query = (turned(query, cosine_ref[...], sine_ref[...]) * HD ** (-0.5)).astype(jnp.bfloat16)
        scores = lax.dot_general(
            query, keys, (((1,), (1,)), ((), ())), preferred_element_type=jnp.float32
        )
        scores = jnp.where(allowed, scores, -jnp.inf)
        highest = jnp.max(scores, axis=-1, keepdims=True)
        powered = jnp.exp(scores - highest)
        softened = (powered / jnp.sum(powered, axis=-1, keepdims=True)).astype(jnp.bfloat16)
        head = jnp.dot(softened, values, preferred_element_type=jnp.float32).astype(jnp.bfloat16)
        mixed.append((head.astype(jnp.float32) * gate))
        names.append(name)
    for e in range(experts):
        out_ref[:, e * HD : (e + 1) * HD] = jnp.where(
            names[0] == float(e), mixed[0], jnp.where(names[1] == float(e), mixed[1], 0.0)
        ).astype(jnp.bfloat16)


def by_head(
    tokens, norm_gain, router, routes, prompt_lengths, wq_train, wo_train, wkv_train, page_table
):
    mp_count = lax.axis_size("mp")
    experts, shard_rows, width = wq_train.shape
    heads = width // HD // mp_count
    own_width = heads * HD
    tok_rows, model_width = tokens.shape
    group_rows = tok_rows * mp_count
    prompt_len = group_rows // 2
    prompt_group = lax.axis_index("dp")

    wide_tokens = tokens.astype(jnp.float32)
    normed = (
        wide_tokens
        * lax.rsqrt(jnp.mean(wide_tokens * wide_tokens, axis=-1, keepdims=True) + 1e-06)
        * norm_gain
    ).astype(jnp.bfloat16)
    segment = lax.all_gather(normed, "mp", axis=0, tiled=True)
    logits = jnp.dot(normed, router, preferred_element_type=jnp.float32)
    labels = jnp.arange(experts, dtype=jnp.int32)[None, :]
    first_logit = jnp.sum(jnp.where(routes[:, 0:1] == labels, logits, 0.0), axis=1)
    second_logit = jnp.sum(jnp.where(routes[:, 1:2] == labels, logits, 0.0), axis=1)
    gate_first = 1.0 / (1.0 + jnp.exp(second_logit - first_logit))
    gate_second = 1.0 / (1.0 + jnp.exp(first_logit - second_logit))
    side = jnp.concatenate(
        [routes.astype(jnp.float32), gate_first[:, None], gate_second[:, None]], axis=1
    )
    side = lax.all_gather(side, "mp", axis=0, tiled=True)
    page_ids = lax.all_gather(page_table[0, 0], "mp", axis=0, tiled=True)

    def by_owner(weights):
        parts = weights.astype(jnp.bfloat16).reshape(experts, shard_rows, mp_count, heads, HD)
        return parts.transpose(2, 1, 3, 0, 4).reshape(mp_count, shard_rows, experts * own_width)

    pair = wkv_train.astype(jnp.bfloat16).reshape(shard_rows, 2, mp_count, own_width)
    pair = pair.transpose(2, 0, 1, 3).reshape(mp_count, shard_rows, 2 * own_width)
    inward = jnp.concatenate([by_owner(wq_train), pair], axis=2)
    inward = lax.all_to_all(inward, "mp", split_axis=0, concat_axis=0, tiled=True)
    inward = lax.all_gather(
        inward.reshape(mp_count * shard_rows, -1), "dp", axis=0, tiled=True
    )
    outward = lax.all_to_all(by_owner(wo_train), "mp", split_axis=0, concat_axis=0, tiled=True)
    outward = lax.all_gather(
        outward.reshape(mp_count * shard_rows, -1), "dp", axis=0, tiled=True
    )

    projected = jnp.dot(segment, inward, preferred_element_type=jnp.float32)

    half = HD // 2
    frequency = 10000.0 ** (-(jnp.arange(half, dtype=jnp.float32) * 2.0 / HD))
    angles = jnp.arange(prompt_len, dtype=jnp.float32)[:, None] * frequency[None, :]
    cosine = jnp.concatenate([jnp.cos(angles)] * 2, axis=1)
    sine = jnp.concatenate([-jnp.sin(angles), jnp.sin(angles)], axis=1)

    cells = jnp.arange(mp_count * mp_count * PCAP, dtype=jnp.int32)
    pages = jnp.arange(page_ids.shape[0], dtype=jnp.int32)
    source = jnp.sum(jnp.where(page_ids[None, :] == cells[:, None], pages[None, :] + 1, 0), 1) - 1
    query_width = experts * own_width
    key_values, pool = pl.pallas_call(
        functools.partial(pages_kernel, heads),
        grid=(1,),
        in_specs=[
            pl.BlockSpec(memory_space=pltpu.SMEM),
            pl.BlockSpec((group_rows, 2 * own_width), lambda i: (0, query_width // (2 * own_width))),
            pl.BlockSpec((group_rows, HD), lambda i: (0, 0)),
            pl.BlockSpec((group_rows, HD), lambda i: (0, 0)),
        ],
        out_specs=[
            pl.BlockSpec((group_rows, 2 * own_width), lambda i: (0, 0)),
            pl.BlockSpec((cells.shape[0] * PAGE, 2 * own_width), lambda i: (0, 0)),
        ],
        out_shape=[
            jax.ShapeDtypeStruct((group_rows, 2 * own_width), jnp.bfloat16),
            jax.ShapeDtypeStruct((cells.shape[0] * PAGE, 2 * own_width), jnp.bfloat16),
        ],
        compiler_params=pltpu.CompilerParams(vmem_limit_bytes=40 * 2**20),
    )(source, projected, jnp.concatenate([cosine] * 2), jnp.concatenate([sine] * 2))
    pool = pool.reshape(mp_count, mp_count * PCAP, PAGE, 2 * own_width)
    pool = lax.all_to_all(pool, "mp", split_axis=0, concat_axis=0, tiled=True)
    pool = pool.reshape(mp_count, mp_count * PCAP, PAGE, 2, own_width).transpose(1, 2, 3, 0, 4)
    pool = pool.reshape(mp_count * PCAP, PAGE, 2 * width)

    lengths = lax.dynamic_slice_in_dim(prompt_lengths, 2 * prompt_group, 2)
    head_width = experts * HD
    mixed = pl.pallas_call(
        functools.partial(attention_kernel, experts),
        grid=(2, heads),
        in_specs=[
            pl.BlockSpec(memory_space=pltpu.SMEM),
            pl.BlockSpec((prompt_len, head_width), lambda p, h: (p, h)),
            pl.BlockSpec((prompt_len, HD), lambda p, h: (p, h)),
            pl.BlockSpec((prompt_len, HD), lambda p, h: (p, heads + h)),
            pl.BlockSpec((prompt_len, HD), lambda p, h: (0, 0)),
            pl.BlockSpec((prompt_len, HD), lambda p, h: (0, 0)),
            pl.BlockSpec((prompt_len, side.shape[1]), lambda p, h: (p, 0)),
        ],
        out_specs=pl.BlockSpec((prompt_len, head_width), lambda p, h: (p, h)),
        out_shape=jax.ShapeDtypeStruct((group_rows, heads * head_width), jnp.bfloat16),
        compiler_params=pltpu.CompilerParams(vmem_limit_bytes=40 * 2**20),
    )(lengths, projected, key_values, key_values, cosine, sine, side)
    partial_value = lax.dot_general(
        mixed, outward, (((1,), (1,)), ((), ())), preferred_element_type=jnp.float32
    ).astype(jnp.bfloat16)
    attended = lax.psum_scatter(partial_value, "mp", scatter_dimension=0, tiled=True)
    return (attended, pool)


def on_device(tokens, norm_gain, router, routes, prompt_lengths, wq_train, *others):
    mp_count = lax.axis_size("mp")
    split_heads = wq_train.shape[0] == mp_count and wq_train.shape[2] // HD % mp_count == 0
    program = by_head if split_heads else by_expert
    return program(tokens, norm_gain, router, routes, prompt_lengths, wq_train, *others)


def solution(mesh):
    placed = (
        P(("dp", "mp"), None),
        P(),
        P(),
        P(("dp", "mp"), None),
        P(),
        P(None, ("dp", "mp"), None),
        P(None, ("dp", "mp"), None),
        P(("dp", "mp"), None),
        P("dp", "mp", None),
    )
    return jax.shard_map(
        on_device,
        mesh=mesh,
        in_specs=placed,
        out_specs=(P(("dp", "mp"), None), P(("dp", "mp"), None, None)),
        check_vma=False,
    )
```

```python
import functools

import jax
import jax.numpy as jnp
from jax import lax
from jax.experimental import pallas as pl
from jax.experimental.pallas import tpu as pltpu
from jax.sharding import PartitionSpec as P

HD = 128
PAGE = 16
PCAP = 2


def rotate(vectors, positions):
    half_dim = vectors.shape[-1] // 2
    frequency = 10000.0 ** (-(jnp.arange(half_dim, dtype=jnp.float32) * 2.0 / vectors.shape[-1]))
    angles = positions.astype(jnp.float32)[:, None] * frequency[None, :]
    cosine = jnp.cos(angles)[:, None, :]
    sine = jnp.sin(angles)[:, None, :]
    leading = vectors[..., :half_dim]
    trailing = vectors[..., half_dim:]
    return jnp.concatenate(
        [leading * cosine - trailing * sine, trailing * cosine + leading * sine], axis=-1
    )


def by_expert(
    tokens, norm_gain, router, routes, prompt_lengths, wq_train, wo_train, wkv_train, page_table
):
    mp_count = lax.axis_size("mp")
    experts = wq_train.shape[0]
    blocks = mp_count // experts
    width = wq_train.shape[2]
    block_width = width // blocks
    head_dim = HD
    block_heads = block_width // head_dim
    tok_rows = tokens.shape[0]
    model_width = tokens.shape[1]
    capacity = tok_rows // 4 + tok_rows // 16
    prompt_len = tok_rows * mp_count // 2
    writer_pages = tok_rows * blocks // PAGE
    slot_count = mp_count * PCAP
    device = lax.axis_index("mp")
    expert = device // blocks
    prompt_group = lax.axis_index("dp")
    shard_rows = wq_train.shape[1]
    query_part = wq_train.reshape(experts, shard_rows, blocks, block_width).transpose(0, 2, 1, 3)
    query_part = query_part.reshape(mp_count, shard_rows, block_width).astype(jnp.bfloat16)
    output_part = wo_train.reshape(experts, shard_rows, blocks, block_width).transpose(0, 2, 1, 3)
    output_part = output_part.reshape(mp_count, shard_rows, block_width).astype(jnp.bfloat16)
    pair_part = wkv_train.reshape(shard_rows, 2, blocks, block_width).transpose(2, 0, 1, 3)
    pair_part = pair_part.reshape(blocks, shard_rows, 2 * block_width)
    pair_part = jnp.broadcast_to(pair_part[None], (experts, blocks, shard_rows, 2 * block_width))
    pair_part = pair_part.reshape(mp_count, shard_rows, 2 * block_width).astype(jnp.bfloat16)
    exchanged = (
        lax.all_to_all(query_part, "mp", split_axis=0, concat_axis=1, tiled=True),
        lax.all_to_all(output_part, "mp", split_axis=0, concat_axis=1, tiled=True),
        lax.all_to_all(pair_part, "mp", split_axis=0, concat_axis=1, tiled=True),
    )
    query_w, output_w, pair_w = (
        lax.all_gather(exchanged[0], "dp", axis=1, tiled=True),
        lax.all_gather(exchanged[1], "dp", axis=1, tiled=True),
        lax.all_gather(exchanged[2], "dp", axis=1, tiled=True),
    )
    query_w = query_w[0]
    output_w = output_w[0]
    pair_w = pair_w[0]
    wide_tokens = tokens.astype(jnp.float32)
    normed = (
        wide_tokens
        * lax.rsqrt(jnp.mean(wide_tokens * wide_tokens, axis=-1, keepdims=True) + 1e-06)
        * norm_gain
    ).astype(jnp.bfloat16)
    logits = jnp.dot(normed, router, preferred_element_type=jnp.float32)
    labels = jnp.arange(experts, dtype=jnp.int32)
    first_hot = routes[:, 0][None, :] == labels[:, None]
    second_hot = routes[:, 1][None, :] == labels[:, None]
    first_logit = jnp.sum(jnp.where(first_hot.T, logits, 0.0), axis=1)
    second_logit = jnp.sum(jnp.where(second_hot.T, logits, 0.0), axis=1)
    gate_first = 1.0 / (1.0 + jnp.exp(second_logit - first_logit))
    gate_second = 1.0 / (1.0 + jnp.exp(first_logit - second_logit))
    gates = jnp.where(
        first_hot, gate_first[None, :], jnp.where(second_hot, gate_second[None, :], 0.0)
    )
    named = first_hot | second_hot
    upto = jnp.arange(tok_rows)[:, None] <= jnp.arange(tok_rows)[None, :]
    ranking = (
        jnp.dot(
            named.astype(jnp.bfloat16),
            upto.astype(jnp.bfloat16),
            preferred_element_type=jnp.float32,
        ).astype(jnp.int32)
        - 1
    )
    chosen = named[:, None, :] & (
        ranking[:, None, :] == jnp.arange(capacity, dtype=jnp.int32)[None, :, None]
    )
    slot_row = jnp.sum(
        jnp.where(chosen, jnp.arange(tok_rows, dtype=jnp.int32)[None, None, :], 0), axis=-1
    )
    filled = jnp.any(chosen, axis=-1)
    picked = jnp.where(filled[..., None], normed[slot_row], jnp.zeros((), jnp.bfloat16))
    outgoing = jnp.broadcast_to(picked[:, None], (experts, blocks, capacity, model_width)).reshape(
        mp_count, capacity, model_width
    )
    places = jnp.where(filled, (device * tok_rows + slot_row) % prompt_len, 0)
    outgoing_places = jnp.broadcast_to(places[:, None], (experts, blocks, capacity)).reshape(
        mp_count, capacity
    )
    arrived = lax.all_to_all(outgoing, "mp", split_axis=0, concat_axis=0, tiled=True)
    arrived_places = lax.all_to_all(outgoing_places, "mp", split_axis=0, concat_axis=0, tiled=True)
    segment = lax.all_gather(normed, "mp", axis=0, tiled=True)
    projected = jnp.dot(segment, pair_w, preferred_element_type=jnp.float32)
    row_places = jnp.arange(segment.shape[0], dtype=jnp.int32) % prompt_len
    keyed = rotate(
        projected[:, :block_width].reshape(-1, block_heads, head_dim), row_places
    ).reshape(-1, block_width)
    kv_rows = jnp.concatenate([keyed, projected[:, block_width:]], axis=1).astype(jnp.bfloat16)
    own_pages = lax.dynamic_slice_in_dim(
        kv_rows, expert * writer_pages * PAGE, writer_pages * PAGE, 0
    )
    own_pages = own_pages.reshape(writer_pages, PAGE, 2 * block_width)
    page_ids = page_table[0, 0]
    target_cells = page_ids // slot_count * PCAP + page_ids % PCAP
    placing = (
        target_cells[None, :] == jnp.arange(mp_count * PCAP, dtype=jnp.int32)[:, None]
    ).astype(jnp.bfloat16)
    outgoing_pages = jnp.einsum(
        "cq,qpk->cpk", placing, own_pages, preferred_element_type=jnp.float32
    ).astype(jnp.bfloat16)
    outgoing_pages = outgoing_pages.reshape(mp_count, PCAP, PAGE, 2 * block_width)
    page_pool = lax.all_to_all(outgoing_pages, "mp", split_axis=0, concat_axis=0, tiled=True)
    queries = jnp.dot(arrived.reshape(-1, model_width), query_w, preferred_element_type=jnp.float32)
    query_places = arrived_places.reshape(-1)
    queries = (
        rotate(queries.reshape(-1, block_heads, head_dim), query_places) * head_dim ** (-0.5)
    ).astype(jnp.bfloat16)
    key_side = (
        kv_rows[:, :block_width].reshape(2, prompt_len, block_heads, head_dim).transpose(0, 2, 1, 3)
    )
    value_side = (
        kv_rows[:, block_width:].reshape(2, prompt_len, block_heads, head_dim).transpose(0, 2, 1, 3)
    )
    key_index = jnp.arange(prompt_len, dtype=jnp.int32)
    half_rows = mp_count // 2 * capacity
    sides = []
    for side in range(2):
        side_places = query_places[side * half_rows : (side + 1) * half_rows]
        length = prompt_lengths[2 * prompt_group + side]
        allowed = (key_index[None, :] <= side_places[:, None]) & (key_index[None, :] < length)
        side_queries = queries[side * half_rows : (side + 1) * half_rows].transpose(1, 0, 2)

        def one_head(operands):
            query_head, key_head, value_head = operands
            scores = lax.dot_general(
                query_head, key_head, (((1,), (1,)), ((), ())), preferred_element_type=jnp.float32
            )
            scores = jnp.where(allowed, scores, -jnp.inf)
            highest = jnp.max(scores, axis=-1, keepdims=True)
            powered = jnp.exp(scores - highest)
            softened = (powered / jnp.sum(powered, axis=-1, keepdims=True)).astype(jnp.bfloat16)
            return jnp.dot(softened, value_head, preferred_element_type=jnp.float32).astype(
                jnp.bfloat16
            )

        sides.append(lax.map(one_head, (side_queries, key_side[side], value_side[side])))
    heads_out = jnp.stack(sides).transpose(0, 2, 1, 3).reshape(2 * half_rows, block_width)
    partial_value = lax.dot_general(
        heads_out, output_w, (((1,), (1,)), ((), ())), preferred_element_type=jnp.float32
    )
    partial_value = partial_value.astype(jnp.bfloat16).reshape(mp_count, capacity, model_width)
    returned = lax.all_to_all(partial_value, "mp", split_axis=0, concat_axis=0, tiled=True)
    page_pool = page_pool.reshape(slot_count, PAGE, 2 * block_width)
    summed = (
        returned.astype(jnp.float32).reshape(experts, blocks, capacity, model_width).sum(axis=1)
    )
    summed = summed.reshape(experts * capacity, model_width)
    weights = jnp.where(chosen, gates[:, None, :], 0.0).reshape(experts * capacity, tok_rows)
    mixed = lax.dot_general(
        weights,
        summed,
        (((0,), (0,)), ((), ())),
        precision=lax.Precision.HIGHEST,
        preferred_element_type=jnp.float32,
    )
    return (mixed.astype(jnp.bfloat16), page_pool)


def turned(vectors, cosine, sine):
    return vectors * cosine + pltpu.roll(vectors, vectors.shape[-1] // 2, 1) * sine


def pages_kernel(heads, source_ref, raw_ref, cosine_ref, sine_ref, kv_ref, pool_ref):
    rows = raw_ref.shape[0]
    width = heads * HD
    for h in range(heads):
        columns = slice(h * HD, (h + 1) * HD)
        kv_ref[:, columns] = turned(
            raw_ref[:, columns], cosine_ref[...], sine_ref[...]
        ).astype(jnp.bfloat16)
    kv_ref[:, width:] = raw_ref[:, width:].astype(jnp.bfloat16)

    def place(cell, carry):
        page = source_ref[cell]
        start = pl.multiple_of(jnp.maximum(page, 0) * PAGE, PAGE)
        content = kv_ref[pl.ds(start, PAGE), :]
        pool_ref[pl.ds(pl.multiple_of(cell * PAGE, PAGE), PAGE), :] = jnp.where(
            page >= 0, content, jnp.zeros_like(content)
        )
        return carry

    lax.fori_loop(0, pool_ref.shape[0] // PAGE, place, 0)


def attention_kernel(
    experts, length_ref, raw_ref, key_ref, value_ref, cosine_ref, sine_ref, side_ref, out_ref
):
    rows = key_ref.shape[0]
    length = length_ref[pl.program_id(0)]
    key_index = lax.broadcasted_iota(jnp.int32, (rows, rows), 1)
    row_index = lax.broadcasted_iota(jnp.int32, (rows, rows), 0)
    allowed = (key_index <= row_index) & (key_index < length)
    keys = key_ref[...]
    values = value_ref[...]
    mixed = []
    names = []
    for choice in range(2):
        name = side_ref[:, choice : choice + 1]
        gate = side_ref[:, 2 + choice : 3 + choice]
        query = jnp.zeros((rows, HD), jnp.float32)
        for e in range(experts):
            query = jnp.where(name == float(e), raw_ref[:, e * HD : (e + 1) * HD], query)
        query = (turned(query, cosine_ref[...], sine_ref[...]) * HD ** (-0.5)).astype(jnp.bfloat16)
        scores = lax.dot_general(
            query, keys, (((1,), (1,)), ((), ())), preferred_element_type=jnp.float32
        )
        scores = jnp.where(allowed, scores, -jnp.inf)
        highest = jnp.max(scores, axis=-1, keepdims=True)
        powered = jnp.exp(scores - highest)
        softened = (powered / jnp.sum(powered, axis=-1, keepdims=True)).astype(jnp.bfloat16)
        head = jnp.dot(softened, values, preferred_element_type=jnp.float32).astype(jnp.bfloat16)
        mixed.append((head.astype(jnp.float32) * gate))
        names.append(name)
    for e in range(experts):
        out_ref[:, e * HD : (e + 1) * HD] = jnp.where(
            names[0] == float(e), mixed[0], jnp.where(names[1] == float(e), mixed[1], 0.0)
        ).astype(jnp.bfloat16)


def pack_kernel(heads, query_ref, output_ref, key_ref, value_ref, inward_ref, outward_ref):
    experts = query_ref.shape[0]
    for h in range(heads):
        for e in range(experts):
            columns = slice((h * experts + e) * HD, (h * experts + e + 1) * HD)
            own = slice(h * HD, (h + 1) * HD)
            inward_ref[0, :, columns] = query_ref[e, :, own].astype(jnp.bfloat16)
            outward_ref[0, :, columns] = output_ref[e, :, own].astype(jnp.bfloat16)
    start = heads * experts * HD
    inward_ref[0, :, start : start + heads * HD] = key_ref[...].astype(jnp.bfloat16)
    inward_ref[0, :, start + heads * HD :] = value_ref[...].astype(jnp.bfloat16)


def greet(peers):
    barrier = pltpu.get_barrier_semaphore()
    for peer in peers:
        pl.semaphore_signal(barrier, inc=1, device_id=peer, device_id_type=pl.DeviceIdType.MESH)
    pl.semaphore_wait(barrier, len(peers))


def exchange_kernel(
    mp_count,
    inward_ref,
    outward_ref,
    normed_ref,
    side_ref,
    table_ref,
    inward_all,
    outward_all,
    normed_all,
    side_all,
    table_all,
    local_sem,
    send_sem,
    recv_sem,
    send_small,
    recv_small,
):
    d = lax.axis_index("dp")
    m = lax.axis_index("mp")
    twin = d + 1 - 2 * lax.rem(d, 2)
    across = lax.rem(d + 2, 4)
    beside = m + 1 - 2 * lax.rem(m, 2)

    def shifted(k):
        return lax.rem(m + k + mp_count, mp_count)

    greet([(d, shifted(k)) for k in range(1, mp_count)] + [(twin, m), (across, m)])
    sent = []

    def send(source, target, sems, place, device):
        copy = pltpu.make_async_remote_copy(
            src_ref=source,
            dst_ref=target,
            send_sem=sems[0].at[place],
            recv_sem=sems[1].at[place],
            device_id=device,
            device_id_type=pl.DeviceIdType.MESH,
        )
        copy.start()
        sent.append(copy)

    def arrived(target, sems, place):
        pltpu.make_async_remote_copy(
            src_ref=target,
            dst_ref=target,
            send_sem=sems[0].at[place],
            recv_sem=sems[1].at[place],
            device_id=(twin, m),
            device_id_type=pl.DeviceIdType.MESH,
        ).wait_recv()

    wide = (send_sem, recv_sem)
    small = (send_small, recv_small)
    parts = (inward_ref, outward_ref)
    wholes = (inward_all, outward_all)
    lines = mp_count // 2
    own = d * mp_count + m
    locals_ = [
        pltpu.make_async_copy(inward_ref.at[m], inward_all.at[own], local_sem.at[0]),
        pltpu.make_async_copy(outward_ref.at[m], outward_all.at[own], local_sem.at[1]),
        pltpu.make_async_copy(normed_ref, normed_all.at[m], local_sem.at[2]),
        pltpu.make_async_copy(side_ref, side_all.at[m], local_sem.at[3]),
        pltpu.make_async_copy(table_ref, table_all.at[m], local_sem.at[4]),
    ]
    for part in range(2):
        for k in range(1, mp_count):
            to = shifted(k)
            send(parts[part].at[to], wholes[part].at[own], wide, (part, 0, k), (d, to))
        if part == 0:
            for k in range(1, lines):
                send(normed_ref, normed_all.at[m], small, (2, k), (d, shifted(2 * k)))
            for k in range(1, mp_count):
                to = shifted(k)
                send(side_ref, side_all.at[m], small, (0, k), (d, to))
                send(table_ref, table_all.at[m], small, (1, k), (d, to))
    for copy in locals_:
        copy.start()

    def relay(part, k):
        slot = across * mp_count + shifted(-k)
        arrived(wholes[part].at[slot], wide, (part, 1, k))
        send(wholes[part].at[slot], wholes[part].at[slot], wide, (part, 3, k), (twin, m))

    steps = [(part, k) for part in range(2) for k in range(mp_count)]
    for i, (part, k) in enumerate(steps):
        slot = d * mp_count + shifted(-k)
        source = parts[part].at[m]
        if k > 0:
            arrived(wholes[part].at[slot], wide, (part, 0, k))
            source = wholes[part].at[slot]
        send(source, wholes[part].at[slot], wide, (part, 1, k), (across, m))
        send(source, wholes[part].at[slot], wide, (part, 2, k), (twin, m))
        if i >= 2:
            relay(*steps[i - 2])
        if part == 0 and k < lines:
            row = shifted(-2 * k)
            block = normed_ref
            if k > 0:
                arrived(normed_all.at[row], small, (2, k))
                block = normed_all.at[row]
            send(block, normed_all.at[row], small, (3, k), (d, beside))
    relay(*steps[-2])
    relay(*steps[-1])
    for part, k in steps:
        arrived(wholes[part].at[twin * mp_count + shifted(-k)], wide, (part, 2, k))
        far = lax.rem(twin + 2, 4)
        arrived(wholes[part].at[far * mp_count + shifted(-k)], wide, (part, 3, k))
    for k in range(lines):
        arrived(normed_all.at[lax.rem(beside - 2 * k + mp_count, mp_count)], small, (3, k))
    for k in range(1, mp_count):
        arrived(side_all.at[shifted(-k)], small, (0, k))
        arrived(table_all.at[shifted(-k)], small, (1, k))
    for copy in sent:
        copy.wait_send()
    for copy in locals_:
        copy.wait()


def return_kernel(
    mp_count,
    partial_ref,
    pool_ref,
    out_ref,
    pool_all,
    pair_in,
    line_out,
    line_in,
    local_sem,
    send_sem,
    recv_sem,
    send_page,
    recv_page,
):
    d = lax.axis_index("dp")
    m = lax.axis_index("mp")
    line = m // 2
    x = lax.rem(m, 2)
    lines = mp_count // 2
    own_width = pool_ref.shape[2] // 2
    width = own_width * mp_count

    def shifted(k):
        return lax.rem(m + k + mp_count, mp_count)

    greet([(d, shifted(k)) for k in range(1, mp_count)])
    sent = []

    def remote(source, target, sends, receives, place, device):
        return pltpu.make_async_remote_copy(
            src_ref=source,
            dst_ref=target,
            send_sem=sends.at[place],
            recv_sem=receives.at[place],
            device_id=device,
            device_id_type=pl.DeviceIdType.MESH,
        )

    def send(*description):
        copy = remote(*description)
        copy.start()
        sent.append(copy)

    beside = (d, line * 2 + 1 - x)
    for k in [*range(1, lines), 0]:
        goal = lax.rem(line + k, lines)
        send(partial_ref.at[goal * 2 + 1 - x], pair_in.at[k], send_sem, recv_sem, (0, k), beside)

    def columns(side, device):
        return pl.ds(pl.multiple_of(side * width + device * own_width, own_width), own_width)

    locals_ = []
    for side in range(2):
        half = pl.ds(side * own_width, own_width)
        locals_.append(
            pltpu.make_async_copy(
                pool_ref.at[m, :, half], pool_all.at[:, columns(side, m)], local_sem.at[side]
            )
        )
        locals_[-1].start()
        for k in range(1, mp_count):
            to = shifted(k)
            send(
                pool_ref.at[to, :, half],
                pool_all.at[:, columns(side, m)],
                send_page,
                recv_page,
                (side, k),
                (d, to),
            )
    for k in range(1, lines):
        goal = lax.rem(line + k, lines)
        remote(pair_in.at[k], pair_in.at[k], send_sem, recv_sem, (0, k), beside).wait_recv()
        line_out[k] = (
            partial_ref[goal * 2 + x].astype(jnp.float32) + pair_in[k].astype(jnp.float32)
        ).astype(jnp.bfloat16)
        send(line_out.at[k], line_in.at[k], send_sem, recv_sem, (1, k), (d, goal * 2 + x))
    remote(pair_in.at[0], pair_in.at[0], send_sem, recv_sem, (0, 0), beside).wait_recv()
    for k in range(1, lines):
        remote(line_in.at[k], line_in.at[k], send_sem, recv_sem, (1, k), beside).wait_recv()
    total = partial_ref[m].astype(jnp.float32) + pair_in[0].astype(jnp.float32)
    for k in range(1, lines):
        total = total + line_in[k].astype(jnp.float32)
    out_ref[...] = total.astype(jnp.bfloat16)
    for side in range(2):
        for k in range(1, mp_count):
            target = pool_all.at[:, columns(side, shifted(-k))]
            remote(target, target, send_page, recv_page, (side, k), beside).wait_recv()
    for copy in sent:
        copy.wait_send()
    for copy in locals_:
        copy.wait()


def by_head(
    tokens, norm_gain, router, routes, prompt_lengths, wq_train, wo_train, wkv_train, page_table
):
    mp_count = lax.axis_size("mp")
    experts, shard_rows, width = wq_train.shape
    heads = width // HD // mp_count
    own_width = heads * HD
    tok_rows, model_width = tokens.shape
    group_rows = tok_rows * mp_count
    prompt_len = group_rows // 2
    prompt_group = lax.axis_index("dp")

    wide_tokens = tokens.astype(jnp.float32)
    normed = (
        wide_tokens
        * lax.rsqrt(jnp.mean(wide_tokens * wide_tokens, axis=-1, keepdims=True) + 1e-06)
        * norm_gain
    ).astype(jnp.bfloat16)
    logits = jnp.dot(normed, router, preferred_element_type=jnp.float32)
    labels = jnp.arange(experts, dtype=jnp.int32)[None, :]
    first_logit = jnp.sum(jnp.where(routes[:, 0:1] == labels, logits, 0.0), axis=1)
    second_logit = jnp.sum(jnp.where(routes[:, 1:2] == labels, logits, 0.0), axis=1)
    gate_first = 1.0 / (1.0 + jnp.exp(second_logit - first_logit))
    gate_second = 1.0 / (1.0 + jnp.exp(first_logit - second_logit))
    side = jnp.concatenate(
        [routes.astype(jnp.float32), gate_first[:, None], gate_second[:, None]], axis=1
    )
    side = jnp.pad(side, ((0, 0), (0, HD - side.shape[1])))
    table = jnp.pad(page_table[0], ((0, 7), (0, HD - page_table.shape[2])))

    inner = experts * own_width
    inward, outward = pl.pallas_call(
        functools.partial(pack_kernel, heads),
        grid=(mp_count,),
        in_specs=[
            pl.BlockSpec((experts, shard_rows, own_width), lambda i: (0, 0, i)),
            pl.BlockSpec((experts, shard_rows, own_width), lambda i: (0, 0, i)),
            pl.BlockSpec((shard_rows, own_width), lambda i: (0, i)),
            pl.BlockSpec((shard_rows, own_width), lambda i: (0, mp_count + i)),
        ],
        out_specs=[
            pl.BlockSpec((1, shard_rows, inner + 2 * own_width), lambda i: (i, 0, 0)),
            pl.BlockSpec((1, shard_rows, inner), lambda i: (i, 0, 0)),
        ],
        out_shape=[
            jax.ShapeDtypeStruct((mp_count, shard_rows, inner + 2 * own_width), jnp.bfloat16),
            jax.ShapeDtypeStruct((mp_count, shard_rows, inner), jnp.bfloat16),
        ],
        compiler_params=pltpu.CompilerParams(vmem_limit_bytes=32 * 2**20),
    )(wq_train, wo_train, wkv_train, wkv_train)
    places = 4 * mp_count
    inward, outward, segment, side, table = pl.pallas_call(
        functools.partial(exchange_kernel, mp_count),
        in_specs=[pl.BlockSpec(memory_space=pl.ANY)] * 5,
        out_specs=[pl.BlockSpec(memory_space=pl.ANY)] * 5,
        out_shape=[
            jax.ShapeDtypeStruct((places, *inward.shape[1:]), jnp.bfloat16),
            jax.ShapeDtypeStruct((places, *outward.shape[1:]), jnp.bfloat16),
            jax.ShapeDtypeStruct((mp_count, *normed.shape), jnp.bfloat16),
            jax.ShapeDtypeStruct((mp_count, *side.shape), jnp.float32),
            jax.ShapeDtypeStruct((mp_count, *table.shape), jnp.int32),
        ],
        scratch_shapes=[
            pltpu.SemaphoreType.DMA((5,)),
            pltpu.SemaphoreType.DMA((2, 4, mp_count)),
            pltpu.SemaphoreType.DMA((2, 4, mp_count)),
            pltpu.SemaphoreType.DMA((4, mp_count)),
            pltpu.SemaphoreType.DMA((4, mp_count)),
        ],
        compiler_params=pltpu.CompilerParams(collective_id=0, has_side_effects=True),
    )(inward, outward, normed, side, table)
    inward = inward.reshape(places * shard_rows, -1)
    outward = outward.reshape(places * shard_rows, -1)
    segment = segment.reshape(group_rows, model_width)
    side = side.reshape(group_rows, HD)
    page_ids = table[:, 0, : page_table.shape[2]].reshape(-1)

    projected = jnp.dot(segment, inward, preferred_element_type=jnp.float32)

    half = HD // 2
    frequency = 10000.0 ** (-(jnp.arange(half, dtype=jnp.float32) * 2.0 / HD))
    angles = jnp.arange(prompt_len, dtype=jnp.float32)[:, None] * frequency[None, :]
    cosine = jnp.concatenate([jnp.cos(angles)] * 2, axis=1)
    sine = jnp.concatenate([-jnp.sin(angles), jnp.sin(angles)], axis=1)

    cells = jnp.arange(mp_count * mp_count * PCAP, dtype=jnp.int32)
    pages = jnp.arange(page_ids.shape[0], dtype=jnp.int32)
    source = jnp.sum(jnp.where(page_ids[None, :] == cells[:, None], pages[None, :] + 1, 0), 1) - 1
    query_width = experts * own_width
    key_values, pool = pl.pallas_call(
        functools.partial(pages_kernel, heads),
        grid=(1,),
        in_specs=[
            pl.BlockSpec(memory_space=pltpu.SMEM),
            pl.BlockSpec((group_rows, 2 * own_width), lambda i: (0, query_width // (2 * own_width))),
            pl.BlockSpec((group_rows, HD), lambda i: (0, 0)),
            pl.BlockSpec((group_rows, HD), lambda i: (0, 0)),
        ],
        out_specs=[
            pl.BlockSpec((group_rows, 2 * own_width), lambda i: (0, 0)),
            pl.BlockSpec((cells.shape[0] * PAGE, 2 * own_width), lambda i: (0, 0)),
        ],
        out_shape=[
            jax.ShapeDtypeStruct((group_rows, 2 * own_width), jnp.bfloat16),
            jax.ShapeDtypeStruct((cells.shape[0] * PAGE, 2 * own_width), jnp.bfloat16),
        ],
        compiler_params=pltpu.CompilerParams(vmem_limit_bytes=40 * 2**20),
    )(source, projected, jnp.concatenate([cosine] * 2), jnp.concatenate([sine] * 2))
    pool_rows = mp_count * PCAP * PAGE
    pool = pool.reshape(mp_count, pool_rows, 2 * own_width)
    lengths = lax.dynamic_slice_in_dim(prompt_lengths, 2 * prompt_group, 2)
    head_width = experts * HD
    mixed = pl.pallas_call(
        functools.partial(attention_kernel, experts),
        grid=(2, heads),
        in_specs=[
            pl.BlockSpec(memory_space=pltpu.SMEM),
            pl.BlockSpec((prompt_len, head_width), lambda p, h: (p, h)),
            pl.BlockSpec((prompt_len, HD), lambda p, h: (p, h)),
            pl.BlockSpec((prompt_len, HD), lambda p, h: (p, heads + h)),
            pl.BlockSpec((prompt_len, HD), lambda p, h: (0, 0)),
            pl.BlockSpec((prompt_len, HD), lambda p, h: (0, 0)),
            pl.BlockSpec((prompt_len, side.shape[1]), lambda p, h: (p, 0)),
        ],
        out_specs=pl.BlockSpec((prompt_len, head_width), lambda p, h: (p, h)),
        out_shape=jax.ShapeDtypeStruct((group_rows, heads * head_width), jnp.bfloat16),
        compiler_params=pltpu.CompilerParams(vmem_limit_bytes=40 * 2**20),
    )(lengths, projected, key_values, key_values, cosine, sine, side)
    partial_value = lax.dot_general(
        mixed, outward, (((1,), (1,)), ((), ())), preferred_element_type=jnp.float32
    ).astype(jnp.bfloat16)
    block = (mp_count // 2, tok_rows, model_width)
    vmem = pl.BlockSpec(memory_space=pltpu.VMEM)
    anywhere = pl.BlockSpec(memory_space=pl.ANY)
    attended, pool = pl.pallas_call(
        functools.partial(return_kernel, mp_count),
        in_specs=[vmem, anywhere],
        out_specs=[vmem, anywhere],
        out_shape=[
            jax.ShapeDtypeStruct((tok_rows, model_width), jnp.bfloat16),
            jax.ShapeDtypeStruct((pool_rows, 2 * width), jnp.bfloat16),
        ],
        scratch_shapes=[
            pltpu.VMEM(block, jnp.bfloat16),
            pltpu.VMEM(block, jnp.bfloat16),
            pltpu.VMEM(block, jnp.bfloat16),
            pltpu.SemaphoreType.DMA((2,)),
            pltpu.SemaphoreType.DMA((2, mp_count // 2)),
            pltpu.SemaphoreType.DMA((2, mp_count // 2)),
            pltpu.SemaphoreType.DMA((2, mp_count)),
            pltpu.SemaphoreType.DMA((2, mp_count)),
        ],
        compiler_params=pltpu.CompilerParams(
            collective_id=1, has_side_effects=True, vmem_limit_bytes=40 * 2**20
        ),
    )(partial_value.reshape(mp_count, tok_rows, model_width), pool)
    return (attended, pool.reshape(mp_count * PCAP, PAGE, 2 * width))


def on_device(tokens, norm_gain, router, routes, prompt_lengths, wq_train, *others):
    mp_count = lax.axis_size("mp")
    split_heads = wq_train.shape[0] == mp_count and lax.axis_size("dp") == 4 and wq_train.shape[2] // HD % mp_count == 0
    program = by_head if split_heads else by_expert
    return program(tokens, norm_gain, router, routes, prompt_lengths, wq_train, *others)


def solution(mesh):
    placed = (
        P(("dp", "mp"), None),
        P(),
        P(),
        P(("dp", "mp"), None),
        P(),
        P(None, ("dp", "mp"), None),
        P(None, ("dp", "mp"), None),
        P(("dp", "mp"), None),
        P("dp", "mp", None),
    )
    return jax.shard_map(
        on_device,
        mesh=mesh,
        in_specs=placed,
        out_specs=(P(("dp", "mp"), None), P(("dp", "mp"), None, None)),
        check_vma=False,
    )
```

```python
import functools

import jax
import jax.numpy as jnp
from jax import lax
from jax.experimental import pallas as pl
from jax.experimental.pallas import tpu as pltpu
from jax.sharding import PartitionSpec as P

HD = 128
PAGE = 16
PCAP = 2
WINDOW = 3
LATE = 4


def rotate(vectors, positions):
    half_dim = vectors.shape[-1] // 2
    frequency = 10000.0 ** (-(jnp.arange(half_dim, dtype=jnp.float32) * 2.0 / vectors.shape[-1]))
    angles = positions.astype(jnp.float32)[:, None] * frequency[None, :]
    cosine = jnp.cos(angles)[:, None, :]
    sine = jnp.sin(angles)[:, None, :]
    leading = vectors[..., :half_dim]
    trailing = vectors[..., half_dim:]
    return jnp.concatenate(
        [leading * cosine - trailing * sine, trailing * cosine + leading * sine], axis=-1
    )


def by_expert(
    tokens, norm_gain, router, routes, prompt_lengths, wq_train, wo_train, wkv_train, page_table
):
    mp_count = lax.axis_size("mp")
    experts = wq_train.shape[0]
    blocks = mp_count // experts
    width = wq_train.shape[2]
    block_width = width // blocks
    head_dim = HD
    block_heads = block_width // head_dim
    tok_rows = tokens.shape[0]
    model_width = tokens.shape[1]
    capacity = tok_rows // 4 + tok_rows // 16
    prompt_len = tok_rows * mp_count // 2
    writer_pages = tok_rows * blocks // PAGE
    slot_count = mp_count * PCAP
    device = lax.axis_index("mp")
    expert = device // blocks
    prompt_group = lax.axis_index("dp")
    shard_rows = wq_train.shape[1]
    query_part = wq_train.reshape(experts, shard_rows, blocks, block_width).transpose(0, 2, 1, 3)
    query_part = query_part.reshape(mp_count, shard_rows, block_width).astype(jnp.bfloat16)
    output_part = wo_train.reshape(experts, shard_rows, blocks, block_width).transpose(0, 2, 1, 3)
    output_part = output_part.reshape(mp_count, shard_rows, block_width).astype(jnp.bfloat16)
    pair_part = wkv_train.reshape(shard_rows, 2, blocks, block_width).transpose(2, 0, 1, 3)
    pair_part = pair_part.reshape(blocks, shard_rows, 2 * block_width)
    pair_part = jnp.broadcast_to(pair_part[None], (experts, blocks, shard_rows, 2 * block_width))
    pair_part = pair_part.reshape(mp_count, shard_rows, 2 * block_width).astype(jnp.bfloat16)
    exchanged = (
        lax.all_to_all(query_part, "mp", split_axis=0, concat_axis=1, tiled=True),
        lax.all_to_all(output_part, "mp", split_axis=0, concat_axis=1, tiled=True),
        lax.all_to_all(pair_part, "mp", split_axis=0, concat_axis=1, tiled=True),
    )
    query_w, output_w, pair_w = (
        lax.all_gather(exchanged[0], "dp", axis=1, tiled=True),
        lax.all_gather(exchanged[1], "dp", axis=1, tiled=True),
        lax.all_gather(exchanged[2], "dp", axis=1, tiled=True),
    )
    query_w = query_w[0]
    output_w = output_w[0]
    pair_w = pair_w[0]
    wide_tokens = tokens.astype(jnp.float32)
    normed = (
        wide_tokens
        * lax.rsqrt(jnp.mean(wide_tokens * wide_tokens, axis=-1, keepdims=True) + 1e-06)
        * norm_gain
    ).astype(jnp.bfloat16)
    logits = jnp.dot(normed, router, preferred_element_type=jnp.float32)
    labels = jnp.arange(experts, dtype=jnp.int32)
    first_hot = routes[:, 0][None, :] == labels[:, None]
    second_hot = routes[:, 1][None, :] == labels[:, None]
    first_logit = jnp.sum(jnp.where(first_hot.T, logits, 0.0), axis=1)
    second_logit = jnp.sum(jnp.where(second_hot.T, logits, 0.0), axis=1)
    gate_first = 1.0 / (1.0 + jnp.exp(second_logit - first_logit))
    gate_second = 1.0 / (1.0 + jnp.exp(first_logit - second_logit))
    gates = jnp.where(
        first_hot, gate_first[None, :], jnp.where(second_hot, gate_second[None, :], 0.0)
    )
    named = first_hot | second_hot
    upto = jnp.arange(tok_rows)[:, None] <= jnp.arange(tok_rows)[None, :]
    ranking = (
        jnp.dot(
            named.astype(jnp.bfloat16),
            upto.astype(jnp.bfloat16),
            preferred_element_type=jnp.float32,
        ).astype(jnp.int32)
        - 1
    )
    chosen = named[:, None, :] & (
        ranking[:, None, :] == jnp.arange(capacity, dtype=jnp.int32)[None, :, None]
    )
    slot_row = jnp.sum(
        jnp.where(chosen, jnp.arange(tok_rows, dtype=jnp.int32)[None, None, :], 0), axis=-1
    )
    filled = jnp.any(chosen, axis=-1)
    picked = jnp.where(filled[..., None], normed[slot_row], jnp.zeros((), jnp.bfloat16))
    outgoing = jnp.broadcast_to(picked[:, None], (experts, blocks, capacity, model_width)).reshape(
        mp_count, capacity, model_width
    )
    places = jnp.where(filled, (device * tok_rows + slot_row) % prompt_len, 0)
    outgoing_places = jnp.broadcast_to(places[:, None], (experts, blocks, capacity)).reshape(
        mp_count, capacity
    )
    arrived = lax.all_to_all(outgoing, "mp", split_axis=0, concat_axis=0, tiled=True)
    arrived_places = lax.all_to_all(outgoing_places, "mp", split_axis=0, concat_axis=0, tiled=True)
    segment = lax.all_gather(normed, "mp", axis=0, tiled=True)
    projected = jnp.dot(segment, pair_w, preferred_element_type=jnp.float32)
    row_places = jnp.arange(segment.shape[0], dtype=jnp.int32) % prompt_len
    keyed = rotate(
        projected[:, :block_width].reshape(-1, block_heads, head_dim), row_places
    ).reshape(-1, block_width)
    kv_rows = jnp.concatenate([keyed, projected[:, block_width:]], axis=1).astype(jnp.bfloat16)
    own_pages = lax.dynamic_slice_in_dim(
        kv_rows, expert * writer_pages * PAGE, writer_pages * PAGE, 0
    )
    own_pages = own_pages.reshape(writer_pages, PAGE, 2 * block_width)
    page_ids = page_table[0, 0]
    target_cells = page_ids // slot_count * PCAP + page_ids % PCAP
    placing = (
        target_cells[None, :] == jnp.arange(mp_count * PCAP, dtype=jnp.int32)[:, None]
    ).astype(jnp.bfloat16)
    outgoing_pages = jnp.einsum(
        "cq,qpk->cpk", placing, own_pages, preferred_element_type=jnp.float32
    ).astype(jnp.bfloat16)
    outgoing_pages = outgoing_pages.reshape(mp_count, PCAP, PAGE, 2 * block_width)
    page_pool = lax.all_to_all(outgoing_pages, "mp", split_axis=0, concat_axis=0, tiled=True)
    queries = jnp.dot(arrived.reshape(-1, model_width), query_w, preferred_element_type=jnp.float32)
    query_places = arrived_places.reshape(-1)
    queries = (
        rotate(queries.reshape(-1, block_heads, head_dim), query_places) * head_dim ** (-0.5)
    ).astype(jnp.bfloat16)
    key_side = (
        kv_rows[:, :block_width].reshape(2, prompt_len, block_heads, head_dim).transpose(0, 2, 1, 3)
    )
    value_side = (
        kv_rows[:, block_width:].reshape(2, prompt_len, block_heads, head_dim).transpose(0, 2, 1, 3)
    )
    key_index = jnp.arange(prompt_len, dtype=jnp.int32)
    half_rows = mp_count // 2 * capacity
    sides = []
    for side in range(2):
        side_places = query_places[side * half_rows : (side + 1) * half_rows]
        length = prompt_lengths[2 * prompt_group + side]
        allowed = (key_index[None, :] <= side_places[:, None]) & (key_index[None, :] < length)
        side_queries = queries[side * half_rows : (side + 1) * half_rows].transpose(1, 0, 2)

        def one_head(operands):
            query_head, key_head, value_head = operands
            scores = lax.dot_general(
                query_head, key_head, (((1,), (1,)), ((), ())), preferred_element_type=jnp.float32
            )
            scores = jnp.where(allowed, scores, -jnp.inf)
            highest = jnp.max(scores, axis=-1, keepdims=True)
            powered = jnp.exp(scores - highest)
            softened = (powered / jnp.sum(powered, axis=-1, keepdims=True)).astype(jnp.bfloat16)
            return jnp.dot(softened, value_head, preferred_element_type=jnp.float32).astype(
                jnp.bfloat16
            )

        sides.append(lax.map(one_head, (side_queries, key_side[side], value_side[side])))
    heads_out = jnp.stack(sides).transpose(0, 2, 1, 3).reshape(2 * half_rows, block_width)
    partial_value = lax.dot_general(
        heads_out, output_w, (((1,), (1,)), ((), ())), preferred_element_type=jnp.float32
    )
    partial_value = partial_value.astype(jnp.bfloat16).reshape(mp_count, capacity, model_width)
    returned = lax.all_to_all(partial_value, "mp", split_axis=0, concat_axis=0, tiled=True)
    page_pool = page_pool.reshape(slot_count, PAGE, 2 * block_width)
    summed = (
        returned.astype(jnp.float32).reshape(experts, blocks, capacity, model_width).sum(axis=1)
    )
    summed = summed.reshape(experts * capacity, model_width)
    weights = jnp.where(chosen, gates[:, None, :], 0.0).reshape(experts * capacity, tok_rows)
    mixed = lax.dot_general(
        weights,
        summed,
        (((0,), (0,)), ((), ())),
        precision=lax.Precision.HIGHEST,
        preferred_element_type=jnp.float32,
    )
    return (mixed.astype(jnp.bfloat16), page_pool)


def turned(vectors, cosine, sine):
    return vectors * cosine + pltpu.roll(vectors, vectors.shape[-1] // 2, 1) * sine


def pages_kernel(heads, source_ref, raw_ref, cosine_ref, sine_ref, kv_ref, pool_ref):
    rows = raw_ref.shape[0]
    width = heads * HD
    for h in range(heads):
        columns = slice(h * HD, (h + 1) * HD)
        kv_ref[:, columns] = turned(
            raw_ref[:, columns], cosine_ref[...], sine_ref[...]
        ).astype(jnp.bfloat16)
    kv_ref[:, width:] = raw_ref[:, width:].astype(jnp.bfloat16)

    def place(cell, carry):
        page = source_ref[cell]
        start = pl.multiple_of(jnp.clip(page, 0, kv_ref.shape[0] // PAGE - 1) * PAGE, PAGE)
        content = kv_ref[pl.ds(start, PAGE), :]
        pool_ref[pl.ds(pl.multiple_of(cell * PAGE, PAGE), PAGE), :] = jnp.where(
            page >= 0, content, jnp.zeros_like(content)
        )
        return carry

    lax.fori_loop(0, pool_ref.shape[0] // PAGE, place, 0)


def attention_kernel(
    experts, length_ref, raw_ref, key_ref, value_ref, cosine_ref, sine_ref, side_ref, out_ref
):
    rows = key_ref.shape[0]
    length = length_ref[pl.program_id(0)]
    key_index = lax.broadcasted_iota(jnp.int32, (rows, rows), 1)
    row_index = lax.broadcasted_iota(jnp.int32, (rows, rows), 0)
    allowed = (key_index <= row_index) & (key_index < length)
    keys = key_ref[...]
    values = value_ref[...]
    mixed = []
    names = []
    for choice in range(2):
        name = side_ref[:, choice : choice + 1]
        gate = side_ref[:, 2 + choice : 3 + choice]
        query = jnp.zeros((rows, HD), jnp.float32)
        for e in range(experts):
            query = jnp.where(name == float(e), raw_ref[:, e * HD : (e + 1) * HD], query)
        query = (turned(query, cosine_ref[...], sine_ref[...]) * HD ** (-0.5)).astype(jnp.bfloat16)
        scores = lax.dot_general(
            query, keys, (((1,), (1,)), ((), ())), preferred_element_type=jnp.float32
        )
        scores = jnp.where(allowed, scores, -jnp.inf)
        highest = jnp.max(scores, axis=-1, keepdims=True)
        powered = jnp.exp(scores - highest)
        softened = (powered / jnp.sum(powered, axis=-1, keepdims=True)).astype(jnp.bfloat16)
        head = jnp.dot(softened, values, preferred_element_type=jnp.float32).astype(jnp.bfloat16)
        mixed.append((head.astype(jnp.float32) * gate))
        names.append(name)
    for e in range(experts):
        out_ref[:, e * HD : (e + 1) * HD] = jnp.where(
            names[0] == float(e), mixed[0], jnp.where(names[1] == float(e), mixed[1], 0.0)
        ).astype(jnp.bfloat16)


def pack_kernel(heads, query_ref, output_ref, key_ref, value_ref, inward_ref, outward_ref):
    experts = query_ref.shape[0]
    for h in range(heads):
        for e in range(experts):
            columns = slice((h * experts + e) * HD, (h * experts + e + 1) * HD)
            own = slice(h * HD, (h + 1) * HD)
            inward_ref[0, :, columns] = query_ref[e, :, own].astype(jnp.bfloat16)
            outward_ref[0, :, columns] = output_ref[e, :, own].astype(jnp.bfloat16)
    start = heads * experts * HD
    inward_ref[0, :, start : start + heads * HD] = key_ref[...].astype(jnp.bfloat16)
    inward_ref[0, :, start + heads * HD :] = value_ref[...].astype(jnp.bfloat16)


def greet(peers):
    barrier = pltpu.get_barrier_semaphore()
    for peer in peers:
        pl.semaphore_signal(barrier, inc=1, device_id=peer, device_id_type=pl.DeviceIdType.MESH)
    pl.semaphore_wait(barrier, len(peers))


def exchange_kernel(
    mp_count,
    inward_ref,
    outward_ref,
    normed_ref,
    side_ref,
    table_ref,
    inward_all,
    outward_all,
    normed_all,
    side_all,
    table_all,
    local_sem,
    send_sem,
    recv_sem,
    send_small,
    recv_small,
    chain_send,
    chain_recv,
    aside_send,
    aside_recv,
):
    d = lax.axis_index("dp")
    m = lax.axis_index("mp")
    twin = d + 1 - 2 * lax.rem(d, 2)
    across = lax.rem(d + 2, 4)
    beside = m + 1 - 2 * lax.rem(m, 2)

    def shifted(k):
        return lax.rem(m + k + mp_count, mp_count)

    greet([(d, shifted(k)) for k in range(1, mp_count)] + [(twin, m), (across, m)])
    sent = []

    def send(source, target, sems, place, device):
        copy = pltpu.make_async_remote_copy(
            src_ref=source,
            dst_ref=target,
            send_sem=sems[0].at[place],
            recv_sem=sems[1].at[place],
            device_id=device,
            device_id_type=pl.DeviceIdType.MESH,
        )
        copy.start()
        sent.append(copy)

    def arrived(target, sems, place):
        pltpu.make_async_remote_copy(
            src_ref=target,
            dst_ref=target,
            send_sem=sems[0].at[place],
            recv_sem=sems[1].at[place],
            device_id=(twin, m),
            device_id_type=pl.DeviceIdType.MESH,
        ).wait_recv()

    wide = (send_sem, recv_sem)
    small = (send_small, recv_small)
    parts = (inward_ref, outward_ref)
    wholes = (inward_all, outward_all)
    lines = mp_count // 2
    own = d * mp_count + m
    locals_ = [
        pltpu.make_async_copy(inward_ref.at[m], inward_all.at[own], local_sem.at[0]),
        pltpu.make_async_copy(outward_ref.at[m], outward_all.at[own], local_sem.at[1]),
        pltpu.make_async_copy(normed_ref, normed_all.at[m], local_sem.at[2]),
        pltpu.make_async_copy(side_ref, side_all.at[m], local_sem.at[3]),
        pltpu.make_async_copy(table_ref, table_all.at[m], local_sem.at[4]),
    ]
    pending = [
        (part, k) for part in range(2) for k in range(1, mp_count)
    ]

    def launch(count):
        for part, k in pending[:count]:
            to = shifted(k)
            send(parts[part].at[to], wholes[part].at[own], wide, (part, 0, k), (d, to))
        del pending[:count]

    line = m // 2
    far_end = lines - 1

    def origin(way, k):
        return shifted(-2 * k) if way == 0 else shifted(2 * k)

    def has(way, k):
        return line >= k if way == 0 else line + k <= far_end

    def goes_on(way):
        return line < far_end if way == 0 else line > 0

    def hop(way, k, block):
        row = origin(way, k)
        return pltpu.make_async_remote_copy(
            src_ref=block,
            dst_ref=normed_all.at[row],
            send_sem=chain_send.at[way, k],
            recv_sem=chain_recv.at[way, k],
            device_id=(d, shifted(2) if way == 0 else shifted(-2)),
            device_id_type=pl.DeviceIdType.MESH,
        )

    def aside(way, k):
        row = origin(way, k)
        return pltpu.make_async_remote_copy(
            src_ref=normed_all.at[row],
            dst_ref=normed_all.at[row],
            send_sem=aside_send.at[way, k],
            recv_sem=aside_recv.at[way, k],
            device_id=(d, beside),
            device_id_type=pl.DeviceIdType.MESH,
        )

    def chain(way, k, block):
        if k == 0:

            @pl.when(goes_on(way))
            def _():
                hop(way, 0, block).start()

            return

        @pl.when(has(way, k))
        def _():
            row = origin(way, k)
            pltpu.make_async_remote_copy(
                src_ref=normed_all.at[row],
                dst_ref=normed_all.at[row],
                send_sem=chain_send.at[way, k - 1],
                recv_sem=chain_recv.at[way, k - 1],
                device_id=(d, beside),
                device_id_type=pl.DeviceIdType.MESH,
            ).wait_recv()
            if k < far_end:

                @pl.when(goes_on(way))
                def _():
                    hop(way, k, normed_all.at[row]).start()

            aside(way, k).start()

    def chain_end(way, k):
        if k == 0:

            @pl.when(goes_on(way))
            def _():
                hop(way, 0, normed_ref).wait_send()

            return

        @pl.when(has(way, k))
        def _():
            row = lax.rem(beside + (-2 * k if way == 0 else 2 * k) + mp_count, mp_count)
            pltpu.make_async_remote_copy(
                src_ref=normed_all.at[row],
                dst_ref=normed_all.at[row],
                send_sem=aside_send.at[way, k],
                recv_sem=aside_recv.at[way, k],
                device_id=(d, beside),
                device_id_type=pl.DeviceIdType.MESH,
            ).wait_recv()
            aside(way, k).wait_send()
            if k < far_end:

                @pl.when(goes_on(way))
                def _():
                    hop(way, k, normed_all.at[origin(way, k)]).wait_send()

    launch(WINDOW)
    for k in range(1, mp_count):
        to = shifted(k)
        send(side_ref, side_all.at[m], small, (0, k), (d, to))
        send(table_ref, table_all.at[m], small, (1, k), (d, to))
    for copy in locals_:
        copy.start()

    def relay(part, k):
        slot = across * mp_count + shifted(-k)
        arrived(wholes[part].at[slot], wide, (part, 1, k))
        send(wholes[part].at[slot], wholes[part].at[slot], wide, (part, 3, k), (twin, m))

    steps = [(part, k) for part in range(2) for k in range(mp_count)]
    for i, (part, k) in enumerate(steps):
        slot = d * mp_count + shifted(-k)
        source = parts[part].at[m]
        if k > 0:
            arrived(wholes[part].at[slot], wide, (part, 0, k))
            source = wholes[part].at[slot]
            launch(1)
        send(source, wholes[part].at[slot], wide, (part, 1, k), (across, m))
        send(source, wholes[part].at[slot], wide, (part, 2, k), (twin, m))
        if i >= 2:
            relay(*steps[i - 2])
        if (part, k) == (1, LATE):
            for way in range(2):
                chain(way, 0, normed_ref)
            send(normed_ref, normed_all.at[m], small, (3, 0), (d, beside))
    relay(*steps[-2])
    relay(*steps[-1])
    for k in range(1, lines):
        for way in range(2):
            chain(way, k, None)
    for part, k in steps:
        arrived(wholes[part].at[twin * mp_count + shifted(-k)], wide, (part, 2, k))
        far = lax.rem(twin + 2, 4)
        arrived(wholes[part].at[far * mp_count + shifted(-k)], wide, (part, 3, k))
    arrived(normed_all.at[beside], small, (3, 0))
    for k in range(lines):
        for way in range(2):
            chain_end(way, k)
    for k in range(1, mp_count):
        arrived(side_all.at[shifted(-k)], small, (0, k))
        arrived(table_all.at[shifted(-k)], small, (1, k))
    for copy in sent:
        copy.wait_send()
    for copy in locals_:
        copy.wait()


def return_kernel(
    mp_count,
    partial_ref,
    pool_ref,
    out_ref,
    pool_all,
    pair_in,
    line_out,
    line_in,
    local_sem,
    send_sem,
    recv_sem,
    send_page,
    recv_page,
):
    d = lax.axis_index("dp")
    m = lax.axis_index("mp")
    line = m // 2
    x = lax.rem(m, 2)
    lines = mp_count // 2
    own_width = pool_ref.shape[2] // 2
    width = own_width * mp_count

    def shifted(k):
        return lax.rem(m + k + mp_count, mp_count)

    greet([(d, shifted(k)) for k in range(1, mp_count)])
    sent = []

    def remote(source, target, sends, receives, place, device):
        return pltpu.make_async_remote_copy(
            src_ref=source,
            dst_ref=target,
            send_sem=sends.at[place],
            recv_sem=receives.at[place],
            device_id=device,
            device_id_type=pl.DeviceIdType.MESH,
        )

    def send(*description):
        copy = remote(*description)
        copy.start()
        sent.append(copy)

    beside = (d, line * 2 + 1 - x)
    for k in [*range(1, lines), 0]:
        goal = lax.rem(line + k, lines)
        send(partial_ref.at[goal * 2 + 1 - x], pair_in.at[k], send_sem, recv_sem, (0, k), beside)

    def columns(side, device):
        return pl.ds(pl.multiple_of(side * width + device * own_width, own_width), own_width)

    locals_ = []
    for side in range(2):
        half = pl.ds(side * own_width, own_width)
        locals_.append(
            pltpu.make_async_copy(
                pool_ref.at[m, :, half], pool_all.at[:, columns(side, m)], local_sem.at[side]
            )
        )
        locals_[-1].start()
        for k in range(1, mp_count):
            to = shifted(k)
            send(
                pool_ref.at[to, :, half],
                pool_all.at[:, columns(side, m)],
                send_page,
                recv_page,
                (side, k),
                (d, to),
            )
    for k in range(1, lines):
        goal = lax.rem(line + k, lines)
        remote(pair_in.at[k], pair_in.at[k], send_sem, recv_sem, (0, k), beside).wait_recv()
        line_out[k] = (
            partial_ref[goal * 2 + x].astype(jnp.float32) + pair_in[k].astype(jnp.float32)
        ).astype(jnp.bfloat16)
        send(line_out.at[k], line_in.at[k], send_sem, recv_sem, (1, k), (d, goal * 2 + x))
    remote(pair_in.at[0], pair_in.at[0], send_sem, recv_sem, (0, 0), beside).wait_recv()
    for k in range(1, lines):
        remote(line_in.at[k], line_in.at[k], send_sem, recv_sem, (1, k), beside).wait_recv()
    total = partial_ref[m].astype(jnp.float32) + pair_in[0].astype(jnp.float32)
    for k in range(1, lines):
        total = total + line_in[k].astype(jnp.float32)
    out_ref[...] = total.astype(jnp.bfloat16)
    for side in range(2):
        for k in range(1, mp_count):
            target = pool_all.at[:, columns(side, shifted(-k))]
            remote(target, target, send_page, recv_page, (side, k), beside).wait_recv()
    for copy in sent:
        copy.wait_send()
    for copy in locals_:
        copy.wait()


def by_head(
    tokens, norm_gain, router, routes, prompt_lengths, wq_train, wo_train, wkv_train, page_table
):
    mp_count = lax.axis_size("mp")
    experts, shard_rows, width = wq_train.shape
    heads = width // HD // mp_count
    own_width = heads * HD
    tok_rows, model_width = tokens.shape
    group_rows = tok_rows * mp_count
    prompt_len = group_rows // 2
    prompt_group = lax.axis_index("dp")

    wide_tokens = tokens.astype(jnp.float32)
    normed = (
        wide_tokens
        * lax.rsqrt(jnp.mean(wide_tokens * wide_tokens, axis=-1, keepdims=True) + 1e-06)
        * norm_gain
    ).astype(jnp.bfloat16)
    logits = jnp.dot(normed, router, preferred_element_type=jnp.float32)
    labels = jnp.arange(experts, dtype=jnp.int32)[None, :]
    first_logit = jnp.sum(jnp.where(routes[:, 0:1] == labels, logits, 0.0), axis=1)
    second_logit = jnp.sum(jnp.where(routes[:, 1:2] == labels, logits, 0.0), axis=1)
    gate_first = 1.0 / (1.0 + jnp.exp(second_logit - first_logit))
    gate_second = 1.0 / (1.0 + jnp.exp(first_logit - second_logit))
    side = jnp.concatenate(
        [routes.astype(jnp.float32), gate_first[:, None], gate_second[:, None]], axis=1
    )
    side = jnp.pad(side, ((0, 0), (0, HD - side.shape[1])))
    table = jnp.pad(page_table[0], ((0, 7), (0, HD - page_table.shape[2])))

    inner = experts * own_width
    inward, outward = pl.pallas_call(
        functools.partial(pack_kernel, heads),
        grid=(mp_count,),
        in_specs=[
            pl.BlockSpec((experts, shard_rows, own_width), lambda i: (0, 0, i)),
            pl.BlockSpec((experts, shard_rows, own_width), lambda i: (0, 0, i)),
            pl.BlockSpec((shard_rows, own_width), lambda i: (0, i)),
            pl.BlockSpec((shard_rows, own_width), lambda i: (0, mp_count + i)),
        ],
        out_specs=[
            pl.BlockSpec((1, shard_rows, inner + 2 * own_width), lambda i: (i, 0, 0)),
            pl.BlockSpec((1, shard_rows, inner), lambda i: (i, 0, 0)),
        ],
        out_shape=[
            jax.ShapeDtypeStruct((mp_count, shard_rows, inner + 2 * own_width), jnp.bfloat16),
            jax.ShapeDtypeStruct((mp_count, shard_rows, inner), jnp.bfloat16),
        ],
        compiler_params=pltpu.CompilerParams(vmem_limit_bytes=32 * 2**20),
    )(wq_train, wo_train, wkv_train, wkv_train)
    places = 4 * mp_count
    inward, outward, segment, side, table = pl.pallas_call(
        functools.partial(exchange_kernel, mp_count),
        in_specs=[pl.BlockSpec(memory_space=pl.ANY)] * 5,
        out_specs=[pl.BlockSpec(memory_space=pl.ANY)] * 5,
        out_shape=[
            jax.ShapeDtypeStruct((places, *inward.shape[1:]), jnp.bfloat16),
            jax.ShapeDtypeStruct((places, *outward.shape[1:]), jnp.bfloat16),
            jax.ShapeDtypeStruct((mp_count, *normed.shape), jnp.bfloat16),
            jax.ShapeDtypeStruct((mp_count, *side.shape), jnp.float32),
            jax.ShapeDtypeStruct((mp_count, *table.shape), jnp.int32),
        ],
        scratch_shapes=[
            pltpu.SemaphoreType.DMA((5,)),
            pltpu.SemaphoreType.DMA((2, 4, mp_count)),
            pltpu.SemaphoreType.DMA((2, 4, mp_count)),
            pltpu.SemaphoreType.DMA((4, mp_count)),
            pltpu.SemaphoreType.DMA((4, mp_count)),
            *[pltpu.SemaphoreType.DMA((2, mp_count // 2))] * 4,
        ],
        compiler_params=pltpu.CompilerParams(collective_id=0, has_side_effects=True),
    )(inward, outward, normed, side, table)
    inward = inward.reshape(places * shard_rows, -1)
    outward = outward.reshape(places * shard_rows, -1)
    segment = segment.reshape(group_rows, model_width)
    side = side.reshape(group_rows, HD)
    page_ids = table[:, 0, : page_table.shape[2]].reshape(-1)

    projected = jnp.dot(segment, inward, preferred_element_type=jnp.float32)

    half = HD // 2
    frequency = 10000.0 ** (-(jnp.arange(half, dtype=jnp.float32) * 2.0 / HD))
    angles = jnp.arange(prompt_len, dtype=jnp.float32)[:, None] * frequency[None, :]
    cosine = jnp.concatenate([jnp.cos(angles)] * 2, axis=1)
    sine = jnp.concatenate([-jnp.sin(angles), jnp.sin(angles)], axis=1)

    cells = jnp.arange(mp_count * mp_count * PCAP, dtype=jnp.int32)
    pages = jnp.arange(page_ids.shape[0], dtype=jnp.int32)
    source = jnp.sum(jnp.where(page_ids[None, :] == cells[:, None], pages[None, :] + 1, 0), 1) - 1
    query_width = experts * own_width
    key_values, pool = pl.pallas_call(
        functools.partial(pages_kernel, heads),
        grid=(1,),
        in_specs=[
            pl.BlockSpec(memory_space=pltpu.SMEM),
            pl.BlockSpec((group_rows, 2 * own_width), lambda i: (0, query_width // (2 * own_width))),
            pl.BlockSpec((group_rows, HD), lambda i: (0, 0)),
            pl.BlockSpec((group_rows, HD), lambda i: (0, 0)),
        ],
        out_specs=[
            pl.BlockSpec((group_rows, 2 * own_width), lambda i: (0, 0)),
            pl.BlockSpec((cells.shape[0] * PAGE, 2 * own_width), lambda i: (0, 0)),
        ],
        out_shape=[
            jax.ShapeDtypeStruct((group_rows, 2 * own_width), jnp.bfloat16),
            jax.ShapeDtypeStruct((cells.shape[0] * PAGE, 2 * own_width), jnp.bfloat16),
        ],
        compiler_params=pltpu.CompilerParams(vmem_limit_bytes=40 * 2**20),
    )(source, projected, jnp.concatenate([cosine] * 2), jnp.concatenate([sine] * 2))
    pool_rows = mp_count * PCAP * PAGE
    pool = pool.reshape(mp_count, pool_rows, 2 * own_width)
    lengths = lax.dynamic_slice_in_dim(prompt_lengths, 2 * prompt_group, 2)
    head_width = experts * HD
    mixed = pl.pallas_call(
        functools.partial(attention_kernel, experts),
        grid=(2, heads),
        in_specs=[
            pl.BlockSpec(memory_space=pltpu.SMEM),
            pl.BlockSpec((prompt_len, head_width), lambda p, h: (p, h)),
            pl.BlockSpec((prompt_len, HD), lambda p, h: (p, h)),
            pl.BlockSpec((prompt_len, HD), lambda p, h: (p, heads + h)),
            pl.BlockSpec((prompt_len, HD), lambda p, h: (0, 0)),
            pl.BlockSpec((prompt_len, HD), lambda p, h: (0, 0)),
            pl.BlockSpec((prompt_len, side.shape[1]), lambda p, h: (p, 0)),
        ],
        out_specs=pl.BlockSpec((prompt_len, head_width), lambda p, h: (p, h)),
        out_shape=jax.ShapeDtypeStruct((group_rows, heads * head_width), jnp.bfloat16),
        compiler_params=pltpu.CompilerParams(vmem_limit_bytes=40 * 2**20),
    )(lengths, projected, key_values, key_values, cosine, sine, side)
    partial_value = lax.dot_general(
        mixed, outward, (((1,), (1,)), ((), ())), preferred_element_type=jnp.float32
    ).astype(jnp.bfloat16)
    block = (mp_count // 2, tok_rows, model_width)
    vmem = pl.BlockSpec(memory_space=pltpu.VMEM)
    anywhere = pl.BlockSpec(memory_space=pl.ANY)
    attended, pool = pl.pallas_call(
        functools.partial(return_kernel, mp_count),
        in_specs=[vmem, anywhere],
        out_specs=[vmem, anywhere],
        out_shape=[
            jax.ShapeDtypeStruct((tok_rows, model_width), jnp.bfloat16),
            jax.ShapeDtypeStruct((pool_rows, 2 * width), jnp.bfloat16),
        ],
        scratch_shapes=[
            pltpu.VMEM(block, jnp.bfloat16),
            pltpu.VMEM(block, jnp.bfloat16),
            pltpu.VMEM(block, jnp.bfloat16),
            pltpu.SemaphoreType.DMA((2,)),
            pltpu.SemaphoreType.DMA((2, mp_count // 2)),
            pltpu.SemaphoreType.DMA((2, mp_count // 2)),
            pltpu.SemaphoreType.DMA((2, mp_count)),
            pltpu.SemaphoreType.DMA((2, mp_count)),
        ],
        compiler_params=pltpu.CompilerParams(
            collective_id=1, has_side_effects=True, vmem_limit_bytes=40 * 2**20
        ),
    )(partial_value.reshape(mp_count, tok_rows, model_width), pool)
    return (attended, pool.reshape(mp_count * PCAP, PAGE, 2 * width))


def on_device(tokens, norm_gain, router, routes, prompt_lengths, wq_train, *others):
    mp_count = lax.axis_size("mp")
    split_heads = wq_train.shape[0] == mp_count and lax.axis_size("dp") == 4 and wq_train.shape[2] // HD % mp_count == 0
    program = by_head if split_heads else by_expert
    return program(tokens, norm_gain, router, routes, prompt_lengths, wq_train, *others)


def solution(mesh):
    placed = (
        P(("dp", "mp"), None),
        P(),
        P(),
        P(("dp", "mp"), None),
        P(),
        P(None, ("dp", "mp"), None),
        P(None, ("dp", "mp"), None),
        P(("dp", "mp"), None),
        P("dp", "mp", None),
    )
    return jax.shard_map(
        on_device,
        mesh=mesh,
        in_specs=placed,
        out_specs=(P(("dp", "mp"), None), P(("dp", "mp"), None, None)),
        check_vma=False,
    )
```
